32 devices in a mesh: section: 4 (over z), expert: 2 (over core), tensor: 4 (over y, x).
Axes of the slice: x: 2, y: 2, z: 4, core: 2. Of those that a mesh axis runs over, the one named last changes fastest.
Arguments:
- tokens: bfloat16 [4096, 6144], P(('section', 'expert'), 'tensor'), may hold values from -6 to 6
- norm_gain: float32 [2, 6144], P(None, 'tensor'), may hold values from 0.5 to 1.5
- router: float32 [2, 6144, 8], P(None, 'tensor'), may hold values from -0.078125 to 0.078125
- w_gate: bfloat16 [4, 2, 6144, 4096], P('section', 'expert', None, 'tensor'), may hold values from -0.078125 to 0.078125
- w_up: bfloat16 [4, 2, 6144, 4096], P('section', 'expert', None, 'tensor'), may hold values from -0.078125 to 0.078125
- w_down: bfloat16 [4, 2, 4096, 6144], P('section', 'expert', 'tensor'), may hold values from -0.0625 to 0.0625
- expert_ids: int32 [2, 4096, 2], P(None, ('section', 'expert')), may hold values from 0 to 7, all different within a row
- lengths: int32 [4, 8], P(None, 'expert'), may hold values from 32 to 128
Outputs:
- encoded: bfloat16 [4096, 6144], P(('section', 'expert'), 'tensor')
The draws below stay inside these ranges and needn't reach their ends.
All inputs are finite; a program needn't handle non-finite values.
Results may differ from the reference program's by a relative error of at most 0.006.
Values may be sent and summed in bfloat16 or wider, within the bound.
No kernel may reach another device: no remote copies, remote signals or barrier semaphores. Data moves between devices by JAX's collectives and lax.ppermute only.
A program may use at most 128 MiB of HBM per device.

```python
import jax
import jax.numpy as jnp
from jax import lax

D = 6144
E = 8
EXP_WIN = 2
FF_WIN = 8192
TOK_DEV = 512
SEQ_LEN = 128
STEPS = 2
CAP = 64
SEQ_DEV = 4
LAYERS = 2
FSPLIT = 1
HALF_W = 4096
FF_DEV = 1024
TOKENS = 4096
N_SECTION = 4
N_EXPERT = 2
N_TENSOR = 4


def plant(values, key, least, largest):
    longest = values.shape.index(max(values.shape))
    spots = []
    for shift in (0, 1):
        where = [jax.random.randint(jax.random.fold_in(key, axis), (), 0, length) for axis, length in enumerate(values.shape)]
        where[longest] = (where[longest] + shift) % values.shape[longest]
        spots.append(tuple(where))
    return values.at[spots[0]].set(least).at[spots[1]].set(largest)


def block_scale(rng, extent, pieces, smallest, high):
    loudness = 1.0
    for axis_at, shards_of in pieces:
        draws = jax.random.uniform(jax.random.fold_in(jax.random.fold_in(rng, 6), axis_at), (shards_of,), jnp.float32, smallest / len(pieces), high / len(pieces))
        loudness = loudness * jnp.repeat(jnp.exp(draws), extent[axis_at] // shards_of).reshape((-1,) + (1,) * (len(extent) - 1 - axis_at))
    return loudness


def picks_of(rng, rows, count, top, lift):
    ranking = jax.random.permutation(jax.random.fold_in(rng, 1), count)
    favour = ranking
    for power in range(3):
        favour = favour * favour // count
    favour = favour * lift // count
    tickets = jax.random.randint(jax.random.fold_in(rng, 2), (rows, count), 0, 4096) + favour
    sure = jax.random.permutation(jax.random.fold_in(rng, 3), rows)[jnp.arange(count) % rows]
    tickets = jnp.where(jnp.arange(rows)[:, None] == sure[None, :], 1 << 14, tickets)
    score = tickets * count + jnp.arange(count)
    return lax.top_k(score.astype(jnp.int32), top)[1].astype(jnp.int32)


def noise(stream_key, extent, scale, most, shards=(), kind=jnp.bfloat16):
    values = jax.random.normal(stream_key, extent, jnp.float32) * scale
    if len(shards) > 0:
        values = block_scale(stream_key, extent, shards, -0.22, 0.18) * values
    return jnp.clip(values, min=-most, max=most).astype(kind)


def setup_inputs(seed: int = 0) -> dict:
    streams_of = jax.random.split(jax.random.key(seed), 9)
    tokens = noise(streams_of[0], (TOKENS, D), 1.0, 6.0, ((0, 8), (1, 4)))
    norm_gain = jnp.clip(1.0 + 0.1 * jax.random.normal(streams_of[1], (LAYERS, D), jnp.float32), 0.5, 1.5)
    router = noise(streams_of[2], (LAYERS, D, E), D ** -0.5, 0.078125, ((1, 4),), jnp.float32)
    w_gate = noise(streams_of[3], (N_SECTION, N_EXPERT, D, HALF_W), D ** -0.5, 0.078125, ((0, 4), (1, 2), (3, 4)))
    w_up = noise(streams_of[4], (N_SECTION, N_EXPERT, D, HALF_W), D ** -0.5, 0.078125, ((0, 4), (1, 2), (3, 4)))
    w_down = noise(streams_of[5], (N_SECTION, N_EXPERT, HALF_W, D), FF_WIN ** -0.5, 0.0625, ((0, 4), (1, 2), (2, 4)))
    expert_ids = picks_of(streams_of[6], STEPS * TOKENS, E, 2, 2048).reshape((STEPS, TOKENS, 2))
    lengths = plant(jax.random.randint(streams_of[7], (N_SECTION, N_EXPERT * SEQ_DEV), SEQ_LEN // 4, SEQ_LEN + 1), jax.random.fold_in(streams_of[7], 1), SEQ_LEN // 4, SEQ_LEN).astype(jnp.int32)
    return {"tokens": tokens, "norm_gain": norm_gain, "router": router, "w_gate": w_gate, "w_up": w_up, "w_down": w_down, "expert_ids": expert_ids, "lengths": lengths}


norm_eps = 1e-05

def route_tables(choice_ids, seq_lens, gate_logits):
    token_count = choice_ids.shape[0]
    expert_range = jnp.arange(E, dtype=jnp.int32)
    match_ids = choice_ids[:, :, None] == expert_range[None, None, :]
    one_hot = match_ids.astype(jnp.float32)
    picked = lax.optimization_barrier(jnp.sum(gate_logits[:, None, :] * one_hot, axis=2))
    first_weight = jax.nn.sigmoid(picked[:, 0] - picked[:, 1])
    second_weight = jax.nn.sigmoid(picked[:, 1] - picked[:, 0])
    dense_gates = first_weight[:, None] * one_hot[:, 0, :] + second_weight[:, None] * one_hot[:, 1, :]
    dense_gates = dense_gates[:, :EXP_WIN]
    positions = jnp.arange(token_count, dtype=jnp.int32)
    live_rows = positions % SEQ_LEN < jnp.repeat(seq_lens, SEQ_LEN, total_repeat_length=token_count)
    named = jnp.any(match_ids, axis=1)[:, :EXP_WIN] & live_rows[:, None]
    named_int = named.astype(jnp.int32)
    earlier = jnp.cumsum(named_int, axis=0) - named_int
    slot_range = jnp.arange(CAP, dtype=jnp.int32)
    placed = named[None, :, :] & (earlier[None, :, :] == slot_range[:, None, None])
    route_table = jnp.transpose(placed.astype(jnp.float32), (2, 0, 1))
    return (route_table, route_table * jnp.transpose(dense_gates)[:, None, :])

def prepare_group(group_rows, seq_lens, choice_ids, gain_row, router_matrix):
    as_float = group_rows.astype(jnp.float32)
    inv_rms = lax.rsqrt(lax.optimization_barrier(jnp.sum(as_float * as_float, axis=1)) / D + norm_eps)
    scaled = as_float * gain_row[None, :]
    normed = (scaled * inv_rms[:, None]).astype(jnp.bfloat16)
    gate_logits = inv_rms[:, None] * jnp.dot(scaled, router_matrix, precision=lax.Precision.HIGHEST)
    route_table, weighted = route_tables(choice_ids, seq_lens, gate_logits)
    return (normed, route_table, weighted)

def expert_apply(packed):
    expert_rows, gate_cols, up_cols, down_rows = packed
    gate_val = jnp.dot(expert_rows, gate_cols, preferred_element_type=jnp.float32)
    up_val = jnp.dot(expert_rows, up_cols, preferred_element_type=jnp.float32)
    hidden = (jax.nn.silu(gate_val) * up_val).astype(jnp.bfloat16)
    row_count = hidden.shape[0]
    hidden_parts = hidden.reshape(row_count, FSPLIT, 2, N_TENSOR, FF_DEV).astype(jnp.float32)
    down_parts = down_rows.reshape(FSPLIT, 2, N_TENSOR, FF_DEV, D).astype(jnp.float32)
    partial_out = jnp.einsum('rfbtk,fbtkd->fbtrd', hidden_parts, down_parts).astype(jnp.bfloat16)
    partial_out = lax.optimization_barrier(partial_out)
    half_out = lax.optimization_barrier(jnp.sum(partial_out.astype(jnp.float32), axis=2)).astype(jnp.bfloat16)
    half_out = lax.optimization_barrier(half_out)
    slab_out = lax.optimization_barrier(jnp.sum(half_out.astype(jnp.float32), axis=1)).astype(jnp.bfloat16)
    slab_out = lax.optimization_barrier(slab_out)
    return lax.optimization_barrier(jnp.sum(slab_out.astype(jnp.float32), axis=0))

def pair_layer(packed):
    pair_rows, pair_lens, pair_ids, gain_row, router_matrix, gate_pair, up_pair, down_pair = packed

    def prepare_batch(batch_rows, batch_lens, batch_ids):
        normed, route_table, weighted = jax.vmap(prepare_group, in_axes=(0, 0, 0, None, None))(batch_rows, batch_lens, batch_ids, gain_row, router_matrix)
        gathered = jnp.einsum('gecr,grd->egcd', route_table, normed.astype(jnp.float32), precision=lax.Precision.HIGHEST).astype(jnp.bfloat16)
        return (gathered, weighted)
    gathered, weighted = jax.vmap(prepare_batch)(pair_rows, pair_lens, pair_ids)
    expert_rows = jnp.transpose(gathered, (1, 0, 2, 3, 4)).reshape(EXP_WIN, 2 * N_EXPERT * CAP, D)
    gate_cols = gate_pair.reshape(2, EXP_WIN, FSPLIT, D, HALF_W).transpose(1, 3, 2, 0, 4).reshape(EXP_WIN, D, FF_WIN)
    up_cols = up_pair.reshape(2, EXP_WIN, FSPLIT, D, HALF_W).transpose(1, 3, 2, 0, 4).reshape(EXP_WIN, D, FF_WIN)
    down_rows = down_pair.reshape(2, EXP_WIN, FSPLIT, HALF_W, D).transpose(1, 2, 0, 3, 4).reshape(EXP_WIN, FF_WIN, D)
    expert_out = lax.map(expert_apply, (expert_rows, gate_cols, up_cols, down_rows))
    expert_out = expert_out.reshape(EXP_WIN, 2, N_EXPERT, CAP, D)
    mixture = jnp.einsum('cgekr,ecgkd->cgrd', weighted, expert_out, precision=lax.Precision.HIGHEST)
    return (pair_rows.astype(jnp.float32) + mixture).astype(jnp.bfloat16)

def reference(tokens, norm_gain, router, w_gate, w_up, w_down, expert_ids, lengths):
    current = tokens.reshape(N_SECTION, N_EXPERT, TOK_DEV, D)
    section_lens = lengths.reshape(N_SECTION, N_EXPERT, SEQ_DEV)
    gate_all = w_gate.reshape(LAYERS, 2, N_EXPERT, D, HALF_W)
    up_all = w_up.reshape(LAYERS, 2, N_EXPERT, D, HALF_W)
    down_all = w_down.reshape(LAYERS, 2, N_EXPERT, HALF_W, D)
    for step_index in range(STEPS):
        step_ids = expert_ids[step_index].reshape(LAYERS, 2, N_EXPERT, TOK_DEV, 2)
        paired = lax.map(pair_layer, (current.reshape(LAYERS, 2, N_EXPERT, TOK_DEV, D), section_lens.reshape(LAYERS, 2, N_EXPERT, SEQ_DEV), step_ids, norm_gain, router, gate_all, up_all, down_all))
        current = paired.reshape(N_SECTION, N_EXPERT, TOK_DEV, D)
        if step_index + 1 < STEPS:
            current = jnp.roll(current, 2, axis=0)
            section_lens = jnp.roll(section_lens, 2, axis=0)
    return current.reshape(TOKENS, D)
```

```python
import functools

import jax
import jax.numpy as jnp
from jax import lax
from jax.experimental import pallas as pl
from jax.experimental.pallas import tpu as pltpu
from jax.sharding import PartitionSpec as P

D = 6144
E = 8
EXP_WIN = 2
SEQ_LEN = 128
CAP = 64
PARTS = 3

norm_eps = 1e-05
VMEM_BYTES = 48 * 1024 * 1024

bf16 = jnp.bfloat16
f32 = jnp.float32


def params():
    return pltpu.CompilerParams(vmem_limit_bytes=VMEM_BYTES)


def swapped(x, dim):
    axis, bit = dim
    return lax.ppermute(x, axis, [(i, i ^ (1 << bit)) for i in range(lax.axis_size(axis))])


def ahead(x, by, cross=False):
    sections, cores = lax.axis_size("section"), lax.axis_size("expert")
    perm = []
    for s in range(sections):
        for c in range(cores):
            there = (s + by) % sections * cores + (c ^ 1 if cross else c)
            perm.append((s * cores + c, there))
    return lax.ppermute(x, ("section", "expert"), perm)


def nt(a, b):
    return lax.dot_general(a, b, (((1,), (1,)), ((), ())), preferred_element_type=f32)


def tn(a, b):
    return lax.dot_general(a, b, (((0,), (0,)), ((), ())), preferred_element_type=f32)


def one_hot_rows(slot_row):
    rows = slot_row.shape[1]
    places = lax.broadcasted_iota(jnp.int32, (CAP, rows), 0).astype(f32)
    return places == slot_row


def prologue_kernel(core, lens, ids_ref, x_ref, slots_ref, own_ref, other_ref):
    rows = ids_ref.shape[1]
    groups_len = rows // SEQ_LEN
    place = lax.broadcasted_iota(jnp.int32, (1, rows), 1)
    me = core[0]
    named = []
    for step in range(2):
        limit = jnp.zeros((1, rows), jnp.int32)
        for q in range(groups_len):
            limit = jnp.where(place // SEQ_LEN == q, lens[step * groups_len + q], limit)
        live = place % SEQ_LEN < limit
        first = ids_ref[2 * step : 2 * step + 1, :]
        second = ids_ref[2 * step + 1 : 2 * step + 2, :]
        for which in range(2):
            expert = me if which == 0 else 1 - me
            hit = ((first == expert) | (second == expert)) & live
            named.append(jnp.where(hit, 1.0, 0.0))
    named.append(jnp.zeros((4, rows), f32))
    named = jnp.concatenate(named, axis=0)
    r = lax.broadcasted_iota(jnp.int32, (rows, rows), 0)
    c = lax.broadcasted_iota(jnp.int32, (rows, rows), 1)
    before = jnp.where(r < c, 1.0, 0.0).astype(bf16)
    earlier = jnp.dot(named.astype(bf16), before, preferred_element_type=f32)
    slots = jnp.where((named > 0.5) & (earlier < CAP), earlier, -1.0)
    slots_ref[...] = slots
    table = jnp.concatenate(
        [one_hot_rows(slots[0:1]), one_hot_rows(slots[1:2])], axis=0
    )
    table = jnp.where(table, 1.0, 0.0).astype(bf16)
    width = x_ref.shape[1] // PARTS
    for p in range(PARTS):
        got = jnp.dot(table, x_ref[:, p * width : (p + 1) * width], preferred_element_type=f32)
        got = got.astype(bf16)
        own_ref[p] = got[:CAP]
        other_ref[p] = got[CAP:]


def prologue(core, lens, ids_rows, x):
    rows, feats = x.shape
    piece = jax.ShapeDtypeStruct((PARTS, CAP, feats // PARTS), bf16)
    return pl.pallas_call(
        prologue_kernel,
        name="prologue",
        out_shape=(jax.ShapeDtypeStruct((8, rows), f32), piece, piece),
        in_specs=[
            pl.BlockSpec(memory_space=pltpu.SMEM),
            pl.BlockSpec(memory_space=pltpu.SMEM),
            pl.BlockSpec(memory_space=pltpu.VMEM),
            pl.BlockSpec(memory_space=pltpu.VMEM),
        ],
        compiler_params=params(),
    )(core, lens, ids_rows, x)


def row_stats(x_bf, gain, router_t):
    r = router_t * gain
    r1 = r.astype(bf16)
    rest = r - r1.astype(f32)
    r2 = rest.astype(bf16)
    r3 = (rest - r2.astype(f32)).astype(bf16)
    logits = (nt(r3, x_bf) + nt(r2, x_bf)) + nt(r1, x_bf)
    xf = x_bf.astype(f32)
    sq = xf * xf
    hi = sq.astype(bf16)
    lo = (sq - hi.astype(f32)).astype(bf16)
    ones = jnp.ones((8, x_bf.shape[1]), bf16)
    return logits, nt(ones, hi) + nt(ones, lo)


def stats_kernel(x_ref, gain_ref, router_ref, out_ref):
    logits, sq = row_stats(x_ref[...], gain_ref[...], router_ref[...])
    out_ref[:8] = logits
    out_ref[8:] = sq


def stats(x, gain_row, router_t):
    return pl.pallas_call(
        stats_kernel,
        name="stats",
        out_shape=jax.ShapeDtypeStruct((16, x.shape[0]), f32),
        compiler_params=params(),
    )(x, gain_row, router_t)


def row_weights(stat, first, second, me):
    inv = lax.rsqrt(stat[8:9] / D + norm_eps)
    logits = stat[:8] * inv
    names = lax.broadcasted_iota(jnp.int32, logits.shape, 0)
    a = jnp.sum(jnp.where(names == first, logits, 0.0), axis=0, keepdims=True)
    b = jnp.sum(jnp.where(names == second, logits, 0.0), axis=0, keepdims=True)
    wa = jax.nn.sigmoid(a - b)
    wb = jax.nn.sigmoid(b - a)
    out = []
    for which in range(2):
        expert = me if which == 0 else 1 - me
        out.append(jnp.where(first == expert, wa, 0.0) + jnp.where(second == expert, wb, 0.0))
    return out


def weight_table(weights, slots):
    parts = []
    for w, slot in zip(weights, slots):
        hot = one_hot_rows(slot)
        hi = w.astype(bf16).astype(f32)
        lo = w - hi
        parts.append(jnp.where(hot, hi, 0.0).astype(bf16))
        parts.append(jnp.where(hot, lo, 0.0).astype(bf16))
    return jnp.concatenate(parts, axis=0)


def stacked(own, other):
    return jnp.concatenate([own, own, other, other], axis=0)


def prepare_kernel(core, stat_ref, ids_ref, slots_ref, next_ref, x_ref, aux_ref, base_ref, mix_ref):
    me = core[0]
    w_own, w_other = row_weights(stat_ref[...], ids_ref[0:1, :], ids_ref[1:2, :], me)
    s_own, s_other = slots_ref[0:1, :], slots_ref[1:2, :]
    aux_ref[...] = jnp.concatenate(
        [w_own, w_other, s_own, s_other, jnp.zeros((4, w_own.shape[1]), f32)], axis=0
    )
    table = weight_table((w_own, w_other), (s_own, s_other))
    pick = jnp.concatenate([one_hot_rows(next_ref[2:3, :]), one_hot_rows(next_ref[3:4, :])], axis=0)
    pick = jnp.where(pick, 1.0, 0.0).astype(bf16)
    mix_ref[...] = nt(pick, table).astype(bf16)
    width = x_ref.shape[1] // PARTS
    for p in range(PARTS):
        got = jnp.dot(pick, x_ref[:, p * width : (p + 1) * width], preferred_element_type=f32)
        base_ref[p] = got.astype(bf16)


def prepare(core, stat, ids_rows, slots, next_slots, x):
    rows, feats = x.shape
    vmem = pl.BlockSpec(memory_space=pltpu.VMEM)
    return pl.pallas_call(
        prepare_kernel,
        name="prepare",
        out_shape=(
            jax.ShapeDtypeStruct((8, rows), f32),
            jax.ShapeDtypeStruct((PARTS, 2 * CAP, feats // PARTS), bf16),
            jax.ShapeDtypeStruct((2 * CAP, 4 * CAP), bf16),
        ),
        in_specs=[pl.BlockSpec(memory_space=pltpu.SMEM)] + [vmem] * 5,
        compiler_params=params(),
    )(core, stat, ids_rows, slots, next_slots, x)


def repick_kernel(mix_ref, base_ref, own_ref, other_ref, to_own_ref, to_other_ref):
    rows = jnp.dot(
        mix_ref[...], stacked(own_ref[...], other_ref[...]), preferred_element_type=f32
    )
    rows = (base_ref[...].astype(f32) + rows).astype(bf16)
    to_own_ref[...] = rows[:CAP]
    to_other_ref[...] = rows[CAP:]


def repick(mix, base, own, other):
    piece = jax.ShapeDtypeStruct(own.shape, bf16)
    return pl.pallas_call(
        repick_kernel, name="repick", out_shape=(piece, piece), compiler_params=params()
    )(mix, base, own, other)


def between_kernel(x_ref, aux_ref, own_ref, other_ref, gain_ref, router_ref, new_ref, stat_ref):
    table = weight_table((aux_ref[0:1, :], aux_ref[1:2, :]), (aux_ref[2:3, :], aux_ref[3:4, :]))
    width = x_ref.shape[1] // PARTS
    logits = None
    for p in range(PARTS):
        cols = slice(p * width, (p + 1) * width)
        mixed = tn(table, stacked(own_ref[p], other_ref[p]))
        new = (x_ref[:, cols].astype(f32) + mixed).astype(bf16)
        new_ref[:, cols] = new
        l, s = row_stats(new, gain_ref[:, cols], router_ref[:, cols])
        logits = l if logits is None else logits + l
        sq = s if p == 0 else sq + s
    stat_ref[:8] = logits
    stat_ref[8:] = sq


def between(x, aux, own, other, gain_row, router_t):
    return pl.pallas_call(
        between_kernel,
        name="between",
        out_shape=(
            jax.ShapeDtypeStruct(x.shape, bf16),
            jax.ShapeDtypeStruct((16, x.shape[0]), f32),
        ),
        compiler_params=params(),
    )(x, aux, own, other, gain_row, router_t)


def last_kernel(core, x_ref, stat_ref, ids_ref, slots_ref, own_ref, other_ref, out_ref):
    me = core[0]
    weights = row_weights(stat_ref[...], ids_ref[2:3, :], ids_ref[3:4, :], me)
    table = weight_table(weights, (slots_ref[2:3, :], slots_ref[3:4, :]))
    width = x_ref.shape[1] // PARTS
    for p in range(PARTS):
        cols = slice(p * width, (p + 1) * width)
        mixed = tn(table, stacked(own_ref[p], other_ref[p]))
        out_ref[:, cols] = (x_ref[:, cols].astype(f32) + mixed).astype(bf16)


def last(core, x, stat, ids_rows, slots, own, other):
    vmem = pl.BlockSpec(memory_space=pltpu.VMEM)
    return pl.pallas_call(
        last_kernel,
        name="last",
        out_shape=jax.ShapeDtypeStruct(x.shape, bf16),
        in_specs=[pl.BlockSpec(memory_space=pltpu.SMEM)] + [vmem] * 6,
        compiler_params=params(),
    )(core, x, stat, ids_rows, slots, own, other)


def cube_orders(slices):
    bits = slices.bit_length() - 1
    dims = [("tensor", b) for b in range(bits)] + [("section", 0)]
    n = len(dims)
    return [[dims[(i + p * max(1, n // PARTS)) % n] for i in range(n)] for p in range(PARTS)]


def gather_cube(blocks, orders):
    held = [b[None] for b in blocks]
    for k in range(len(orders[0])):
        came = [swapped(held[p], orders[p][k]) for p in range(PARTS)]
        held = [jnp.concatenate([held[p], came[p]], axis=0) for p in range(PARTS)]
    return held


def sum_cube(keep, send, orders):
    keep = [k.astype(f32) for k in keep]
    rounds = len(orders[0])
    for k in range(rounds - 1, -1, -1):
        came = [swapped(send[p], orders[p][k]).astype(f32) for p in range(PARTS)]
        total = [keep[p] + came[p] for p in range(PARTS)]
        half = total[0].shape[0] // 2
        if k > 0:
            send = [t[half:].astype(bf16) for t in total]
            keep = [t[:half] for t in total]
    return [t[0].astype(bf16) for t in total]


def block_place(order, slices, r, z):
    place = 0
    for k, (axis, bit) in enumerate(order):
        on = z if axis == "section" else (r >> bit) & 1
        place |= on << k
    return place


def block_place_traced(order, r, z):
    place = 0
    for k, (axis, bit) in enumerate(order):
        on = z if axis == "section" else (r >> bit) & 1
        place = place + (on << k)
    return place


def experts_kernel(slices, orders, me, *refs):
    ins = refs[: 2 * PARTS]
    gain_ref, gate_ref, up_ref, down_ref = refs[2 * PARTS : 2 * PARTS + 4]
    outs = refs[2 * PARTS + 4 : 4 * PARTS + 4]
    gate_acc, up_acc, sq_acc, hidden = refs[4 * PARTS + 4 :]
    step = pl.program_id(0)
    chunks = PARTS * slices
    rows = ins[0].shape[1]

    @pl.when(step == 0)
    def _():
        gate_acc[...] = jnp.zeros_like(gate_acc)
        up_acc[...] = jnp.zeros_like(up_acc)
        sq_acc[...] = jnp.zeros_like(sq_acc)

    for p in range(PARTS):

        @pl.when((step >= p * slices) & (step < (p + 1) * slices))
        def _():
            x = jnp.concatenate([ins[2 * p][0], ins[2 * p + 1][0]], axis=0).astype(f32)
            sq_acc[...] += jnp.sum(x * x, axis=1, keepdims=True)
            xg = (x * gain_ref[0]).astype(bf16)
            gate_acc[...] += jnp.dot(xg, gate_ref[...], preferred_element_type=f32)
            up_acc[...] += jnp.dot(xg, up_ref[...], preferred_element_type=f32)

    @pl.when(step == chunks - 1)
    def _():
        inv = lax.rsqrt(sq_acc[...] / D + norm_eps)
        gate = gate_acc[...] * inv
        up = up_acc[...] * inv
        hidden[...] = (gate / (1.0 + jnp.exp(-gate)) * up).astype(bf16)

    for p in range(PARTS):

        @pl.when((step >= chunks + p * slices) & (step < chunks + (p + 1) * slices))
        def _():
            r = step - (chunks + p * slices)
            out = jnp.dot(hidden[...], down_ref[...], preferred_element_type=f32).astype(bf16)
            half = outs[2 * p].shape[0]
            for z in range(2):
                place = block_place_traced(orders[p], r, z)
                block = out[z * rows : (z + 1) * rows]
                if orders[p][-1][0] == "section":
                    outs[2 * p + z][place - z * half] = block
                else:

                    @pl.when(place < half)
                    def _():
                        outs[2 * p][place] = block

                    @pl.when(place >= half)
                    def _():
                        outs[2 * p + 1][place - half] = block


def experts(me, held, gain_all, gate_w, up_w, down_w, orders):
    blocks, rows, width = held[0].shape
    slices = blocks // 2
    chunks = PARTS * slices
    hidden_count = gate_w.shape[1]

    def part_and_slice(chunk):
        return chunk // slices, chunk % slices

    def row_map(p, z):
        def index(step, me):
            r = jnp.clip(step - p * slices, 0, slices - 1)
            return (block_place_traced(orders[p], r, z), 0, 0)

        return index

    def weight_place(chunk, me):
        p, r = part_and_slice(chunk)
        return (me[0] ^ r) * PARTS + p

    def in_map(step, me):
        return (weight_place(jnp.minimum(step, chunks - 1), me), 0)

    def gain_map(step, me):
        return (weight_place(jnp.minimum(step, chunks - 1), me), 0, 0)

    def down_map(step, me):
        return (0, weight_place(jnp.maximum(step - chunks, 0), me))

    in_specs = []
    operands = []
    for p in range(PARTS):
        for z in range(2):
            in_specs.append(pl.BlockSpec((1, rows, width), row_map(p, z)))
            operands.append(held[p])
    in_specs += [
        pl.BlockSpec((1, 1, width), gain_map),
        pl.BlockSpec((width, hidden_count), in_map),
        pl.BlockSpec((width, hidden_count), in_map),
        pl.BlockSpec((hidden_count, width), down_map),
    ]
    out_shape = [jax.ShapeDtypeStruct((blocks // 2, rows, width), bf16)] * (2 * PARTS)
    out_specs = [
        pl.BlockSpec((blocks // 2, rows, width), lambda step, me: (0, 0, 0))
    ] * (2 * PARTS)
    flops = 2 * 2 * rows * D * hidden_count * 3
    outs = pl.pallas_call(
        functools.partial(experts_kernel, slices, orders),
        name="experts",
        out_shape=out_shape,
        grid_spec=pltpu.PrefetchScalarGridSpec(
            num_scalar_prefetch=1,
            grid=(2 * chunks,),
            in_specs=in_specs,
            out_specs=out_specs,
            scratch_shapes=[
                pltpu.VMEM((2 * rows, hidden_count), f32),
                pltpu.VMEM((2 * rows, hidden_count), f32),
                pltpu.VMEM((2 * rows, 1), f32),
                pltpu.VMEM((2 * rows, hidden_count), bf16),
            ],
        ),
        compiler_params=params(),
        cost_estimate=pl.CostEstimate(
            flops=flops,
            bytes_accessed=3 * D * hidden_count * 2 + 4 * rows * D * 2,
            transcendentals=2 * rows * hidden_count,
        ),
    )(me, *operands, gain_all, gate_w, up_w, down_w)
    return outs[0::2], outs[1::2]


def tensor_sum(stat):
    for b in range(lax.axis_size("tensor").bit_length() - 1):
        stat = stat + swapped(stat, ("tensor", b))
    return stat


def on_device(tokens, norm_gain, router, w_gate, w_up, w_down, expert_ids, lengths):
    sections = lax.axis_size("section")
    slices = lax.axis_size("tensor")
    section = lax.axis_index("section")
    core = lax.axis_index("expert").astype(jnp.int32)[None]
    me = lax.axis_index("tensor").astype(jnp.int32)[None]
    layer = section // 2
    rows, feats = tokens.shape
    width = feats // PARTS
    across = ("expert", 0)

    gain_row = lax.dynamic_index_in_dim(norm_gain, layer, 0, keepdims=True)
    router_t = lax.dynamic_index_in_dim(router, layer, 0, keepdims=False).T
    ids_rows = jnp.transpose(expert_ids, (0, 2, 1)).reshape(4, rows)
    lens = jnp.concatenate(
        [
            lax.dynamic_index_in_dim(lengths, section, 0, keepdims=False),
            lax.dynamic_index_in_dim(lengths, (section - 2) % sections, 0, keepdims=False),
        ]
    )
    gain_all = lax.all_gather(gain_row[0], "tensor", axis=0, tiled=True)
    gain_all = gain_all.reshape(slices * PARTS, 1, width)
    orders = cube_orders(slices)
    gate_w, up_w, down_w = w_gate[0, 0], w_up[0, 0], w_down[0, 0]

    slots, own, other = prologue(core, lens, ids_rows, tokens)
    block = jnp.concatenate([own, swapped(other, across)], axis=1)
    held = gather_cube([block[p] for p in range(PARTS)], orders)

    far_tokens = ahead(tokens, 2)
    next_slots = ahead(slots, -2)
    stat = tensor_sum(stats(tokens, gain_row, router_t))
    aux, base, mix = prepare(core, stat, ids_rows, slots, next_slots, tokens)
    far_aux = ahead(aux, 2)

    keep, send = experts(me, held, gain_all, gate_w, up_w, down_w, orders)
    summed = sum_cube(keep, send, orders)

    mine = [s[:CAP] for s in summed]
    theirs = [swapped(s[CAP:], across) for s in summed]
    blocks = []
    for p in range(PARTS):
        to_own, to_other = repick(mix, base[p], mine[p], theirs[p])
        blocks.append(jnp.concatenate([ahead(to_own, 2), ahead(to_other, 2, True)], axis=0))
    held = gather_cube(blocks, orders)

    moved = ahead(jnp.stack([jnp.stack(mine), jnp.stack(theirs)]), 2)
    state, stat = between(far_tokens, far_aux, moved[0], moved[1], gain_row, router_t)
    stat = tensor_sum(stat)

    keep, send = experts(me, held, gain_all, gate_w, up_w, down_w, orders)
    summed = sum_cube(keep, send, orders)
    mine = jnp.stack([s[:CAP] for s in summed])
    theirs = swapped(jnp.stack([s[CAP:] for s in summed]), across)
    return last(core, state, stat, ids_rows, slots, mine, theirs)


def solution(mesh):
    in_specs = (
        P(("section", "expert"), "tensor"),
        P(None, "tensor"),
        P(None, "tensor", None),
        P("section", "expert", None, "tensor"),
        P("section", "expert", None, "tensor"),
        P("section", "expert", "tensor", None),
        P(None, ("section", "expert"), None),
        P(None, "expert"),
    )
    out_specs = P(("section", "expert"), "tensor")
    return jax.shard_map(
        on_device, mesh=mesh, in_specs=in_specs, out_specs=out_specs, check_vma=False
    )
```

```python
import functools

import jax
import jax.numpy as jnp
from jax import lax
from jax.experimental import pallas as pl
from jax.experimental.pallas import tpu as pltpu
from jax.sharding import PartitionSpec as P

D = 6144
E = 8
EXP_WIN = 2
SEQ_LEN = 128
CAP = 64
PARTS = 3

norm_eps = 1e-05
VMEM_BYTES = 10 * 1024 * 1024

bf16 = jnp.bfloat16
f32 = jnp.float32


def params():
    return pltpu.CompilerParams(vmem_limit_bytes=VMEM_BYTES)


def swapped(x, dim):
    axis, bit = dim
    return lax.ppermute(x, axis, [(i, i ^ (1 << bit)) for i in range(lax.axis_size(axis))])


def ahead(x, by, cross=False):
    sections, cores = lax.axis_size("section"), lax.axis_size("expert")
    perm = []
    for s in range(sections):
        for c in range(cores):
            there = (s + by) % sections * cores + (c ^ 1 if cross else c)
            perm.append((s * cores + c, there))
    return lax.ppermute(x, ("section", "expert"), perm)


def nt(a, b):
    return lax.dot_general(a, b, (((1,), (1,)), ((), ())), preferred_element_type=f32)


def tn(a, b):
    return lax.dot_general(a, b, (((0,), (0,)), ((), ())), preferred_element_type=f32)


def one_hot_rows(slot_row):
    rows = slot_row.shape[1]
    places = lax.broadcasted_iota(jnp.int32, (CAP, rows), 0).astype(f32)
    return places == slot_row


def prologue_kernel(core, lens, ids_ref, x_ref, slots_ref, own_ref, other_ref):
    rows = ids_ref.shape[1]
    groups_len = rows // SEQ_LEN
    place = lax.broadcasted_iota(jnp.int32, (1, rows), 1)
    me = core[0]
    named = []
    for step in range(2):
        limit = jnp.zeros((1, rows), jnp.int32)
        for q in range(groups_len):
            limit = jnp.where(place // SEQ_LEN == q, lens[step * groups_len + q], limit)
        live = place % SEQ_LEN < limit
        first = ids_ref[2 * step : 2 * step + 1, :]
        second = ids_ref[2 * step + 1 : 2 * step + 2, :]
        for which in range(2):
            expert = me if which == 0 else 1 - me
            hit = ((first == expert) | (second == expert)) & live
            named.append(jnp.where(hit, 1.0, 0.0))
    named.append(jnp.zeros((4, rows), f32))
    named = jnp.concatenate(named, axis=0)
    r = lax.broadcasted_iota(jnp.int32, (rows, rows), 0)
    c = lax.broadcasted_iota(jnp.int32, (rows, rows), 1)
    before = jnp.where(r < c, 1.0, 0.0).astype(bf16)
    earlier = jnp.dot(named.astype(bf16), before, preferred_element_type=f32)
    slots = jnp.where((named > 0.5) & (earlier < CAP), earlier, -1.0)
    slots_ref[...] = slots
    table = jnp.concatenate(
        [one_hot_rows(slots[0:1]), one_hot_rows(slots[1:2])], axis=0
    )
    table = jnp.where(table, 1.0, 0.0).astype(bf16)
    width = x_ref.shape[1] // PARTS
    for p in range(PARTS):
        got = jnp.dot(table, x_ref[:, p * width : (p + 1) * width], preferred_element_type=f32)
        got = got.astype(bf16)
        own_ref[p] = got[:CAP]
        other_ref[p] = got[CAP:]


def prologue(core, lens, ids_rows, x):
    rows, feats = x.shape
    piece = jax.ShapeDtypeStruct((PARTS, CAP, feats // PARTS), bf16)
    return pl.pallas_call(
        prologue_kernel,
        name="prologue",
        out_shape=(jax.ShapeDtypeStruct((8, rows), f32), piece, piece),
        in_specs=[
            pl.BlockSpec(memory_space=pltpu.SMEM),
            pl.BlockSpec(memory_space=pltpu.SMEM),
            pl.BlockSpec(memory_space=pltpu.VMEM),
            pl.BlockSpec(memory_space=pltpu.VMEM),
        ],
        compiler_params=params(),
    )(core, lens, ids_rows, x)


def row_stats(x_bf, gain, router_t):
    r = router_t * gain
    r1 = r.astype(bf16)
    rest = r - r1.astype(f32)
    r2 = rest.astype(bf16)
    r3 = (rest - r2.astype(f32)).astype(bf16)
    logits = (nt(r3, x_bf) + nt(r2, x_bf)) + nt(r1, x_bf)
    xf = x_bf.astype(f32)
    sq = xf * xf
    hi = sq.astype(bf16)
    lo = (sq - hi.astype(f32)).astype(bf16)
    ones = jnp.ones((8, x_bf.shape[1]), bf16)
    return logits, nt(ones, hi) + nt(ones, lo)


def stats_kernel(x_ref, gain_ref, router_ref, out_ref):
    logits, sq = row_stats(x_ref[...], gain_ref[...], router_ref[...])
    out_ref[:8] = logits
    out_ref[8:] = sq


def stats(x, gain_row, router_t):
    return pl.pallas_call(
        stats_kernel,
        name="stats",
        out_shape=jax.ShapeDtypeStruct((16, x.shape[0]), f32),
        compiler_params=params(),
    )(x, gain_row, router_t)


def row_weights(stat, first, second, me):
    inv = lax.rsqrt(stat[8:9] / D + norm_eps)
    logits = stat[:8] * inv
    names = lax.broadcasted_iota(jnp.int32, logits.shape, 0)
    a = jnp.sum(jnp.where(names == first, logits, 0.0), axis=0, keepdims=True)
    b = jnp.sum(jnp.where(names == second, logits, 0.0), axis=0, keepdims=True)
    wa = jax.nn.sigmoid(a - b)
    wb = jax.nn.sigmoid(b - a)
    out = []
    for which in range(2):
        expert = me if which == 0 else 1 - me
        out.append(jnp.where(first == expert, wa, 0.0) + jnp.where(second == expert, wb, 0.0))
    return out


def weight_table(weights, slots):
    parts = []
    for w, slot in zip(weights, slots):
        hot = one_hot_rows(slot)
        hi = w.astype(bf16).astype(f32)
        lo = w - hi
        parts.append(jnp.where(hot, hi, 0.0).astype(bf16))
        parts.append(jnp.where(hot, lo, 0.0).astype(bf16))
    return jnp.concatenate(parts, axis=0)


def stacked(own, other):
    return jnp.concatenate([own, own, other, other], axis=0)


def prepare_kernel(core, stat_ref, ids_ref, slots_ref, next_ref, x_ref, aux_ref, base_ref, mix_ref):
    me = core[0]
    w_own, w_other = row_weights(stat_ref[...], ids_ref[0:1, :], ids_ref[1:2, :], me)
    s_own, s_other = slots_ref[0:1, :], slots_ref[1:2, :]
    aux_ref[...] = jnp.concatenate(
        [w_own, w_other, s_own, s_other, jnp.zeros((4, w_own.shape[1]), f32)], axis=0
    )
    table = weight_table((w_own, w_other), (s_own, s_other))
    pick = jnp.concatenate([one_hot_rows(next_ref[2:3, :]), one_hot_rows(next_ref[3:4, :])], axis=0)
    pick = jnp.where(pick, 1.0, 0.0).astype(bf16)
    mix_ref[...] = nt(pick, table).astype(bf16)
    width = x_ref.shape[1] // PARTS
    for p in range(PARTS):
        got = jnp.dot(pick, x_ref[:, p * width : (p + 1) * width], preferred_element_type=f32)
        base_ref[p] = got.astype(bf16)


def prepare(core, stat, ids_rows, slots, next_slots, x):
    rows, feats = x.shape
    vmem = pl.BlockSpec(memory_space=pltpu.VMEM)
    return pl.pallas_call(
        prepare_kernel,
        name="prepare",
        out_shape=(
            jax.ShapeDtypeStruct((8, rows), f32),
            jax.ShapeDtypeStruct((PARTS, 2 * CAP, feats // PARTS), bf16),
            jax.ShapeDtypeStruct((2 * CAP, 4 * CAP), bf16),
        ),
        in_specs=[pl.BlockSpec(memory_space=pltpu.SMEM)] + [vmem] * 5,
        compiler_params=params(),
    )(core, stat, ids_rows, slots, next_slots, x)


def repick_kernel(mix_ref, base_ref, own_ref, other_ref, to_own_ref, to_other_ref):
    rows = jnp.dot(
        mix_ref[...], stacked(own_ref[...], other_ref[...]), preferred_element_type=f32
    )
    rows = (base_ref[...].astype(f32) + rows).astype(bf16)
    to_own_ref[...] = rows[:CAP]
    to_other_ref[...] = rows[CAP:]


def repick(mix, base, own, other):
    piece = jax.ShapeDtypeStruct(own.shape, bf16)
    return pl.pallas_call(
        repick_kernel, name="repick", out_shape=(piece, piece), compiler_params=params()
    )(mix, base, own, other)


def between_kernel(x_ref, aux_ref, own_ref, other_ref, gain_ref, router_ref, new_ref, stat_ref):
    table = weight_table((aux_ref[0:1, :], aux_ref[1:2, :]), (aux_ref[2:3, :], aux_ref[3:4, :]))
    width = x_ref.shape[1] // PARTS
    logits = None
    for p in range(PARTS):
        cols = slice(p * width, (p + 1) * width)
        mixed = tn(table, stacked(own_ref[p], other_ref[p]))
        new = (x_ref[:, cols].astype(f32) + mixed).astype(bf16)
        new_ref[:, cols] = new
        l, s = row_stats(new, gain_ref[:, cols], router_ref[:, cols])
        logits = l if logits is None else logits + l
        sq = s if p == 0 else sq + s
    stat_ref[:8] = logits
    stat_ref[8:] = sq


def between(x, aux, own, other, gain_row, router_t):
    return pl.pallas_call(
        between_kernel,
        name="between",
        out_shape=(
            jax.ShapeDtypeStruct(x.shape, bf16),
            jax.ShapeDtypeStruct((16, x.shape[0]), f32),
        ),
        compiler_params=params(),
    )(x, aux, own, other, gain_row, router_t)


def last_kernel(core, x_ref, stat_ref, ids_ref, slots_ref, own_ref, other_ref, out_ref):
    me = core[0]
    weights = row_weights(stat_ref[...], ids_ref[2:3, :], ids_ref[3:4, :], me)
    table = weight_table(weights, (slots_ref[2:3, :], slots_ref[3:4, :]))
    width = x_ref.shape[1] // PARTS
    for p in range(PARTS):
        cols = slice(p * width, (p + 1) * width)
        mixed = tn(table, stacked(own_ref[p], other_ref[p]))
        out_ref[:, cols] = (x_ref[:, cols].astype(f32) + mixed).astype(bf16)


def last(core, x, stat, ids_rows, slots, own, other):
    vmem = pl.BlockSpec(memory_space=pltpu.VMEM)
    return pl.pallas_call(
        last_kernel,
        name="last",
        out_shape=jax.ShapeDtypeStruct(x.shape, bf16),
        in_specs=[pl.BlockSpec(memory_space=pltpu.SMEM)] + [vmem] * 6,
        compiler_params=params(),
    )(core, x, stat, ids_rows, slots, own, other)


def cube_orders(slices):
    bits = slices.bit_length() - 1
    dims = [("tensor", b) for b in range(bits)] + [("section", 0)]
    n = len(dims)
    return [[dims[(i + p * max(1, n // PARTS)) % n] for i in range(n)] for p in range(PARTS)]


def tied(x, *before):
    return lax.optimization_barrier((x, before))[0]


def link_users(orders, k, dim):
    return [p for p in range(PARTS) if orders[p][k] == dim]


def join_kernel(a_ref, b_ref, out_ref):
    half = a_ref.shape[0]
    out_ref[:half] = a_ref[...]
    out_ref[half:] = b_ref[...]


def join(a, b):
    return pl.pallas_call(
        join_kernel,
        name="join",
        out_shape=jax.ShapeDtypeStruct((2 * a.shape[0],) + a.shape[1:], a.dtype),
        compiler_params=params(),
    )(a, b)


def readied(values, came, orders, k, last_k, before):
    out = []
    for p in range(PARTS):
        deps = [] if came is None else [came[q] for q in link_users(orders, last_k, orders[p][k])]
        deps = deps + list(before[1])
        if orders[p][k][0] == "section":
            deps = deps + list(before[0])
        out.append(tied(values[p], *deps) if deps else values[p])
    return out


def gather_cube(blocks, orders, before, shadow=None):
    held = [b[None] for b in blocks]
    came = None
    rounds = len(orders[0])
    for k in range(rounds):
        ready = readied(held, came, orders, k, k - 1, before.get(k, ((), ())))
        came = [swapped(ready[p], orders[p][k]) for p in range(PARTS)]
        if k < rounds - 1:
            held = [join(held[p], came[p]) for p in range(PARTS)]
    return held, came


def sum_cube(keep, send, orders, before):
    keep = [k.astype(f32) for k in keep]
    rounds = len(orders[0])
    came = None
    for k in range(rounds - 1, -1, -1):
        turn = rounds - 1 - k
        ready = readied(send, came, orders, k, k + 1, before.get(turn, ((), ())))
        came = [swapped(ready[p], orders[p][k]) for p in range(PARTS)]
        total = [keep[p] + came[p].astype(f32) for p in range(PARTS)]
        half = total[0].shape[0] // 2
        if k > 0:
            send = [t[half:].astype(bf16) for t in total]
            keep = [t[:half] for t in total]
    return [t[0].astype(bf16) for t in total]


def block_place(order, r, z):
    place = 0
    for k, (axis, bit) in enumerate(order):
        on = z if axis == "section" else (r >> bit) & 1
        place = place + (on << k)
    return place


IN_CUTS = 4
AHEAD = 5


def experts_kernel(slices, orders, me, *refs):
    early, late = refs[:PARTS], refs[PARTS : 2 * PARTS]
    gain_ref, gate_ref, up_ref, down_ref = refs[2 * PARTS : 2 * PARTS + 4]
    refs = refs[2 * PARTS + 4 :]
    outs = refs[: 2 * PARTS]
    scaled, hidden, in_w, down_w, in_sems, down_sems = refs[2 * PARTS :]
    rows, width = early[0].shape[1:]
    half = early[0].shape[0]
    mine = me[0]
    depth, tile = in_w.shape[1:]
    tiles = hidden.shape[1] // tile
    chunks = slices * PARTS

    copies = []
    for n in range(tiles):
        for src in (gate_ref, up_ref):
            for q in range(IN_CUTS):
                i = len(copies)
                copies.append(
                    pltpu.make_async_copy(
                        src.at[q * depth : (q + 1) * depth, n * tile : (n + 1) * tile],
                        in_w.at[i],
                        in_sems.at[i],
                    )
                )
    firsts = len(copies)
    for p in range(PARTS):
        for r in range(slices):
            col = pl.multiple_of(((mine ^ r) * PARTS + p) * width, width)
            i = p * slices + r
            copies.append(
                pltpu.make_async_copy(
                    down_ref.at[:, pl.ds(col, width)], down_w.at[i], down_sems.at[i]
                )
            )
    for copy in copies[:AHEAD]:
        copy.start()

    def arrived(i):
        copies[i].wait()
        if i + AHEAD < len(copies):
            copies[i + AHEAD].start()

    squares = jnp.zeros((2 * rows, 128), f32)
    for p in range(PARTS):
        for r in range(slices):
            got = []
            for z in range(2):
                place = block_place(orders[p], r, z)
                got.append(early[p][place] if place < half else late[p][place - half])
            x = jnp.concatenate(got, axis=0).astype(f32)
            scaled[(mine ^ r) * PARTS + p] = (x * gain_ref[r, p]).astype(bf16)
            for c in range(0, width, 128):
                squares = squares + x[:, c : c + 128] * x[:, c : c + 128]
    inv = lax.rsqrt(jnp.sum(squares, axis=1, keepdims=True) / D + norm_eps)

    def product(first):
        total = None
        per = chunks // IN_CUTS
        for q in range(IN_CUTS):
            arrived(first + q)
            for j in range(per):
                term = jnp.dot(
                    scaled[q * per + j],
                    in_w[first + q, j * width : (j + 1) * width, :],
                    preferred_element_type=f32,
                )
                total = term if total is None else total + term
        return total * inv

    for n in range(tiles):
        gate = product(2 * n * IN_CUTS)
        up = product((2 * n + 1) * IN_CUTS)
        hidden[:, n * tile : (n + 1) * tile] = (gate / (1.0 + jnp.exp(-gate)) * up).astype(bf16)

    for p in range(PARTS):
        for r in range(slices):
            arrived(firsts + p * slices + r)
            out = jnp.dot(
                hidden[...], down_w[p * slices + r], preferred_element_type=f32
            ).astype(bf16)
            for z in range(2):
                place = block_place(orders[p], r, z)
                block = out[z * rows : (z + 1) * rows]
                if place < half:
                    outs[2 * p][place] = block
                else:
                    outs[2 * p + 1][place - half] = block


def experts(me, early, late, gain_all, gate_w, up_w, down_w, orders):
    half, rows, width = early[0].shape
    hidden_count = gate_w.shape[1]
    tile = min(512, hidden_count)
    firsts = 2 * (hidden_count // tile) * IN_CUTS
    vmem = pl.BlockSpec(memory_space=pltpu.VMEM)
    hbm = pl.BlockSpec(memory_space=pltpu.HBM)
    outs = pl.pallas_call(
        functools.partial(experts_kernel, half, orders),
        name="experts",
        out_shape=[jax.ShapeDtypeStruct((half, rows, width), bf16)] * (2 * PARTS),
        in_specs=[pl.BlockSpec(memory_space=pltpu.SMEM)]
        + [vmem] * (2 * PARTS + 1)
        + [hbm] * 3,
        out_specs=[vmem] * (2 * PARTS),
        scratch_shapes=[
            pltpu.VMEM((half * PARTS, 2 * rows, width), bf16),
            pltpu.VMEM((2 * rows, hidden_count), bf16),
            pltpu.VMEM((firsts, D // IN_CUTS, tile), bf16),
            pltpu.VMEM((half * PARTS, hidden_count, width), bf16),
            pltpu.SemaphoreType.DMA((firsts,)),
            pltpu.SemaphoreType.DMA((half * PARTS,)),
        ],
        compiler_params=pltpu.CompilerParams(vmem_limit_bytes=47 * 1024 * 1024),
        cost_estimate=pl.CostEstimate(
            flops=2 * 2 * rows * D * hidden_count * 3,
            bytes_accessed=3 * D * hidden_count * 2 + 4 * rows * D * 2,
            transcendentals=2 * rows * hidden_count,
        ),
    )(me, *early, *late, gain_all, gate_w, up_w, down_w)
    return outs[0::2], outs[1::2]


def tensor_sum(stat):
    for b in range(lax.axis_size("tensor").bit_length() - 1):
        stat = stat + swapped(stat, ("tensor", b))
    return stat


def on_device(tokens, norm_gain, router, w_gate, w_up, w_down, expert_ids, lengths):
    sections = lax.axis_size("section")
    slices = lax.axis_size("tensor")
    section = lax.axis_index("section")
    core = lax.axis_index("expert").astype(jnp.int32)[None]
    me = lax.axis_index("tensor").astype(jnp.int32)[None]
    layer = section // 2
    rows, feats = tokens.shape
    width = feats // PARTS
    across = ("expert", 0)

    gain_row = lax.dynamic_index_in_dim(norm_gain, layer, 0, keepdims=True)
    router_t = lax.dynamic_index_in_dim(router, layer, 0, keepdims=False).T
    ids_rows = jnp.transpose(expert_ids, (0, 2, 1)).reshape(4, rows)
    lens = jnp.concatenate(
        [
            lax.dynamic_index_in_dim(lengths, section, 0, keepdims=False),
            lax.dynamic_index_in_dim(lengths, (section - 2) % sections, 0, keepdims=False),
        ]
    )
    gain_all = gain_row.reshape(1, PARTS, 1, width)
    for b in range(slices.bit_length() - 1):
        gain_all = jnp.concatenate([gain_all, swapped(gain_all, ("tensor", b))], axis=0)
    orders = cube_orders(slices)
    rounds = len(orders[0])
    gate_w, up_w, down_w = w_gate[0, 0], w_up[0, 0], w_down[0, 0]
    pieces = []
    begin = 0
    for share in (6, 6, 7, 6, 7):
        pieces.append(tokens[begin : begin + rows * share // 32])
        begin += rows * share // 32

    slots, own, other = prologue(core, lens, ids_rows, tokens)
    far = [ahead(pieces[0], 2)]
    far.append(ahead(tied(pieces[1], far[0]), 2))
    block = jnp.concatenate([own, swapped(other, across)], axis=1)
    waits = {1: ([far[0]], []), rounds - 1: ([far[1]], [gain_all])}
    early, late = gather_cube([block[p] for p in range(PARTS)], orders, waits)

    far.append(ahead(tied(pieces[2], *late), 2))
    next_slots = ahead(slots, -2)
    stat = tensor_sum(stats(tokens, gain_row, router_t))
    aux, base, mix = prepare(core, stat, ids_rows, slots, next_slots, tokens)
    far_aux = ahead(aux, 2)

    keep, send = experts(me, early, late, gain_all, gate_w, up_w, down_w, orders)
    far.append(ahead(tied(pieces[3], *send), 2))
    summed = sum_cube(keep, send, orders, {0: ([], [far[2]]), rounds - 1: ([far[3]], [])})

    mine = [s[:CAP] for s in summed]
    theirs = [swapped(s[CAP:], across) for s in summed]
    blocks = []
    for p in range(PARTS):
        to_own, to_other = repick(mix, base[p], mine[p], theirs[p])
        blocks.append(jnp.concatenate([ahead(to_own, 2), ahead(to_other, 2, True)], axis=0))
    slab_own = ahead(tied(jnp.stack(mine), *blocks), 2)
    slab_other = ahead(tied(jnp.stack(theirs), slab_own), 2)
    waits = {rounds - 2: ([slab_own], []), rounds - 1: ([slab_other], [])}
    early, late = gather_cube(blocks, orders, waits)
    far.append(ahead(tied(pieces[4], slab_other, *late), 2))

    keep, send = experts(me, early, late, gain_all, gate_w, up_w, down_w, orders)
    far_tokens = jnp.concatenate(far, axis=0)
    state, stat = between(far_tokens, far_aux, slab_own, slab_other, gain_row, router_t)
    stat = tensor_sum(stat)
    summed = sum_cube(keep, send, orders, {0: ([], [far[4]]), rounds - 1: ([], [stat])})
    mine = jnp.stack([s[:CAP] for s in summed])
    theirs = swapped(jnp.stack([s[CAP:] for s in summed]), across)
    return last(core, state, stat, ids_rows, slots, mine, theirs)


def solution(mesh):
    in_specs = (
        P(("section", "expert"), "tensor"),
        P(None, "tensor"),
        P(None, "tensor", None),
        P("section", "expert", None, "tensor"),
        P("section", "expert", None, "tensor"),
        P("section", "expert", "tensor", None),
        P(None, ("section", "expert"), None),
        P(None, "expert"),
    )
    out_specs = P(("section", "expert"), "tensor")
    return jax.shard_map(
        on_device, mesh=mesh, in_specs=in_specs, out_specs=out_specs, check_vma=False
    )
```

```python
import functools

import jax
import jax.numpy as jnp
from jax import lax
from jax.experimental import pallas as pl
from jax.experimental.pallas import tpu as pltpu
from jax.sharding import PartitionSpec as P

D = 6144
E = 8
EXP_WIN = 2
SEQ_LEN = 128
CAP = 64
IN_PARTS = 3
OUT_PARTS = 3

norm_eps = 1e-05
VMEM_BYTES = 10 * 1024 * 1024

bf16 = jnp.bfloat16
f32 = jnp.float32


def params():
    return pltpu.CompilerParams(vmem_limit_bytes=VMEM_BYTES)


def cuts(feats, parts):
    ends = [feats // 128 * p // parts * 128 for p in range(parts + 1)]
    return list(zip(ends[:-1], ends[1:]))


def in_cuts(feats):
    units = feats // 128
    first = max(1, units // 6)
    second = (units - first) // 2
    ends = [0, first * 128, (first + second) * 128, feats]
    return list(zip(ends[:-1], ends[1:]))


def swapped(x, dim):
    axis, bit = dim
    return lax.ppermute(x, axis, [(i, i ^ (1 << bit)) for i in range(lax.axis_size(axis))])


def ahead(x, by, cross=False):
    sections, cores = lax.axis_size("section"), lax.axis_size("expert")
    perm = []
    for s in range(sections):
        for c in range(cores):
            there = (s + by) % sections * cores + (c ^ 1 if cross else c)
            perm.append((s * cores + c, there))
    return lax.ppermute(x, ("section", "expert"), perm)


def nt(a, b):
    return lax.dot_general(a, b, (((1,), (1,)), ((), ())), preferred_element_type=f32)


def tn(a, b):
    return lax.dot_general(a, b, (((0,), (0,)), ((), ())), preferred_element_type=f32)


def one_hot_rows(slot_row):
    rows = slot_row.shape[1]
    places = lax.broadcasted_iota(jnp.int32, (CAP, rows), 0).astype(f32)
    return places == slot_row


def prologue_kernel(core, lens, ids_ref, x_ref, slots_ref, own_ref, other_ref):
    rows = ids_ref.shape[1]
    groups_len = rows // SEQ_LEN
    place = lax.broadcasted_iota(jnp.int32, (1, rows), 1)
    me = core[0]
    named = []
    for step in range(2):
        limit = jnp.zeros((1, rows), jnp.int32)
        for q in range(groups_len):
            limit = jnp.where(place // SEQ_LEN == q, lens[step * groups_len + q], limit)
        live = place % SEQ_LEN < limit
        first = ids_ref[2 * step : 2 * step + 1, :]
        second = ids_ref[2 * step + 1 : 2 * step + 2, :]
        for which in range(2):
            expert = me if which == 0 else 1 - me
            hit = ((first == expert) | (second == expert)) & live
            named.append(jnp.where(hit, 1.0, 0.0))
    named.append(jnp.zeros((4, rows), f32))
    named = jnp.concatenate(named, axis=0)
    r = lax.broadcasted_iota(jnp.int32, (rows, rows), 0)
    c = lax.broadcasted_iota(jnp.int32, (rows, rows), 1)
    before = jnp.where(r < c, 1.0, 0.0).astype(bf16)
    earlier = jnp.dot(named.astype(bf16), before, preferred_element_type=f32)
    slots = jnp.where((named > 0.5) & (earlier < CAP), earlier, -1.0)
    slots_ref[...] = slots
    table = jnp.concatenate(
        [one_hot_rows(slots[0:1]), one_hot_rows(slots[1:2])], axis=0
    )
    table = jnp.where(table, 1.0, 0.0).astype(bf16)
    for a, b in cuts(x_ref.shape[1], OUT_PARTS):
        got = jnp.dot(table, x_ref[:, a:b], preferred_element_type=f32).astype(bf16)
        own_ref[:, a:b] = got[:CAP]
        other_ref[:, a:b] = got[CAP:]


def prologue(core, lens, ids_rows, x):
    rows, feats = x.shape
    piece = jax.ShapeDtypeStruct((CAP, feats), bf16)
    return pl.pallas_call(
        prologue_kernel,
        name="prologue",
        out_shape=(jax.ShapeDtypeStruct((8, rows), f32), piece, piece),
        in_specs=[
            pl.BlockSpec(memory_space=pltpu.SMEM),
            pl.BlockSpec(memory_space=pltpu.SMEM),
            pl.BlockSpec(memory_space=pltpu.VMEM),
            pl.BlockSpec(memory_space=pltpu.VMEM),
        ],
        compiler_params=params(),
    )(core, lens, ids_rows, x)


def in_three(v):
    first = v.astype(bf16)
    rest = v - first.astype(f32)
    second = rest.astype(bf16)
    return first, second, (rest - second.astype(f32)).astype(bf16)


def row_stats(x_bf, gain, router_t):
    parts = jnp.concatenate(in_three(router_t * gain), axis=0)
    got = nt(parts, x_bf)
    logits = (got[16:] + got[8:16]) + got[:8]
    xf = x_bf.astype(f32)
    squares = xf[:, :128] * xf[:, :128]
    for c in range(128, xf.shape[1], 128):
        squares = squares + xf[:, c : c + 128] * xf[:, c : c + 128]
    ones = jnp.ones((8, 128), bf16)
    first, second, third = in_three(squares)
    return logits, (nt(ones, third) + nt(ones, second)) + nt(ones, first)


def stats_kernel(x_ref, gain_ref, router_ref, out_ref):
    logits, sq = row_stats(x_ref[...], gain_ref[...], router_ref[...])
    out_ref[:8] = logits
    out_ref[8:] = sq


def stats(x, gain_row, router_t):
    return pl.pallas_call(
        stats_kernel,
        name="stats",
        out_shape=jax.ShapeDtypeStruct((16, x.shape[0]), f32),
        compiler_params=params(),
    )(x, gain_row, router_t)


def row_weights(stat, first, second, me):
    inv = lax.rsqrt(stat[8:9] / D + norm_eps)
    logits = stat[:8] * inv
    names = lax.broadcasted_iota(jnp.int32, logits.shape, 0)
    a = jnp.sum(jnp.where(names == first, logits, 0.0), axis=0, keepdims=True)
    b = jnp.sum(jnp.where(names == second, logits, 0.0), axis=0, keepdims=True)
    wa = jax.nn.sigmoid(a - b)
    wb = jax.nn.sigmoid(b - a)
    out = []
    for which in range(2):
        expert = me if which == 0 else 1 - me
        out.append(jnp.where(first == expert, wa, 0.0) + jnp.where(second == expert, wb, 0.0))
    return out


def weight_table(weights, slots):
    parts = []
    for w, slot in zip(weights, slots):
        hot = one_hot_rows(slot)
        hi = w.astype(bf16).astype(f32)
        lo = w - hi
        parts.append(jnp.where(hot, hi, 0.0).astype(bf16))
        parts.append(jnp.where(hot, lo, 0.0).astype(bf16))
    return jnp.concatenate(parts, axis=0)


def stacked(own, other):
    return jnp.concatenate([own, own, other, other], axis=0)


def prepare_kernel(core, stat_ref, ids_ref, slots_ref, next_ref, x_ref, aux_ref, base_ref, mix_ref):
    me = core[0]
    w_own, w_other = row_weights(stat_ref[...], ids_ref[0:1, :], ids_ref[1:2, :], me)
    s_own, s_other = slots_ref[0:1, :], slots_ref[1:2, :]
    aux_ref[...] = jnp.concatenate(
        [w_own, w_other, s_own, s_other, jnp.zeros((4, w_own.shape[1]), f32)], axis=0
    )
    table = weight_table((w_own, w_other), (s_own, s_other))
    pick = jnp.concatenate([one_hot_rows(next_ref[2:3, :]), one_hot_rows(next_ref[3:4, :])], axis=0)
    pick = jnp.where(pick, 1.0, 0.0).astype(bf16)
    mix_ref[...] = nt(pick, table).astype(bf16)
    for a, b in cuts(x_ref.shape[1], OUT_PARTS):
        got = jnp.dot(pick, x_ref[:, a:b], preferred_element_type=f32)
        base_ref[:, a:b] = got.astype(bf16)


def prepare(core, stat, ids_rows, slots, next_slots, x):
    rows, feats = x.shape
    vmem = pl.BlockSpec(memory_space=pltpu.VMEM)
    return pl.pallas_call(
        prepare_kernel,
        name="prepare",
        out_shape=(
            jax.ShapeDtypeStruct((8, rows), f32),
            jax.ShapeDtypeStruct((2 * CAP, feats), bf16),
            jax.ShapeDtypeStruct((2 * CAP, 4 * CAP), bf16),
        ),
        in_specs=[pl.BlockSpec(memory_space=pltpu.SMEM)] + [vmem] * 5,
        compiler_params=params(),
    )(core, stat, ids_rows, slots, next_slots, x)


def repick_kernel(mix_ref, base_ref, *refs):
    own, other = refs[:OUT_PARTS], refs[OUT_PARTS : 2 * OUT_PARTS]
    to_own_ref, to_other_ref, own_ref, other_ref = refs[2 * OUT_PARTS :]
    for p, (a, b) in enumerate(cuts(base_ref.shape[1], OUT_PARTS)):
        rows = jnp.dot(
            mix_ref[...], stacked(own[p][...], other[p][...]), preferred_element_type=f32
        )
        rows = (base_ref[:, a:b].astype(f32) + rows).astype(bf16)
        to_own_ref[:, a:b] = rows[:CAP]
        to_other_ref[:, a:b] = rows[CAP:]
        own_ref[:, a:b] = own[p][...]
        other_ref[:, a:b] = other[p][...]


def repick(mix, base, own, other):
    piece = jax.ShapeDtypeStruct((CAP, base.shape[1]), bf16)
    return pl.pallas_call(
        repick_kernel, name="repick", out_shape=(piece,) * 4, compiler_params=params()
    )(mix, base, *own, *other)


def lay_kernel(own_ref, other_ref, *outs):
    for out, (a, b) in zip(outs, in_cuts(own_ref.shape[1])):
        out[0, :CAP] = own_ref[:, a:b]
        out[0, CAP:] = other_ref[:, a:b]


def lay(own, other):
    return pl.pallas_call(
        lay_kernel,
        name="lay",
        out_shape=[
            jax.ShapeDtypeStruct((1, 2 * CAP, b - a), bf16)
            for a, b in in_cuts(own.shape[1])
        ],
        compiler_params=params(),
    )(own, other)


def between_kernel(x_ref, aux_ref, own_ref, other_ref, gain_ref, router_ref, new_ref, stat_ref):
    table = weight_table((aux_ref[0:1, :], aux_ref[1:2, :]), (aux_ref[2:3, :], aux_ref[3:4, :]))
    logits = None
    for a, b in cuts(x_ref.shape[1], OUT_PARTS):
        cols = slice(a, b)
        mixed = tn(table, stacked(own_ref[:, cols], other_ref[:, cols]))
        new = (x_ref[:, cols].astype(f32) + mixed).astype(bf16)
        new_ref[:, cols] = new
        l, s = row_stats(new, gain_ref[:, cols], router_ref[:, cols])
        logits = l if logits is None else logits + l
        sq = s if a == 0 else sq + s
    stat_ref[:8] = logits
    stat_ref[8:] = sq


def between(x, aux, own, other, gain_row, router_t):
    return pl.pallas_call(
        between_kernel,
        name="between",
        out_shape=(
            jax.ShapeDtypeStruct(x.shape, bf16),
            jax.ShapeDtypeStruct((16, x.shape[0]), f32),
        ),
        compiler_params=params(),
    )(x, aux, own, other, gain_row, router_t)


def last_kernel(core, x_ref, stat_ref, ids_ref, slots_ref, *refs):
    own, other, out_ref = refs[:OUT_PARTS], refs[OUT_PARTS : 2 * OUT_PARTS], refs[-1]
    me = core[0]
    weights = row_weights(stat_ref[...], ids_ref[2:3, :], ids_ref[3:4, :], me)
    table = weight_table(weights, (slots_ref[2:3, :], slots_ref[3:4, :]))
    for p, (a, b) in enumerate(cuts(x_ref.shape[1], OUT_PARTS)):
        cols = slice(a, b)
        mixed = tn(table, stacked(own[p][...], other[p][...]))
        out_ref[:, cols] = (x_ref[:, cols].astype(f32) + mixed).astype(bf16)


def last(core, x, stat, ids_rows, slots, own, other):
    vmem = pl.BlockSpec(memory_space=pltpu.VMEM)
    return pl.pallas_call(
        last_kernel,
        name="last",
        out_shape=jax.ShapeDtypeStruct(x.shape, bf16),
        in_specs=[pl.BlockSpec(memory_space=pltpu.SMEM)] + [vmem] * (4 + 2 * OUT_PARTS),
        compiler_params=params(),
    )(core, x, stat, ids_rows, slots, *own, *other)


def out_orders(slices):
    bits = slices.bit_length() - 1
    dims = [("tensor", b) for b in range(bits)] + [("section", 0)]
    n = len(dims)
    return [[dims[(i + p * max(1, n // OUT_PARTS)) % n] for i in range(n)] for p in range(OUT_PARTS)]


def tied(x, *before):
    return lax.optimization_barrier((x, before))[0]


def join_kernel(a_ref, b_ref, out_ref):
    half = a_ref.shape[0]
    out_ref[:half] = a_ref[...]
    out_ref[half:] = b_ref[...]


def join(a, b):
    return pl.pallas_call(
        join_kernel,
        name="join",
        out_shape=jax.ShapeDtypeStruct((2 * a.shape[0],) + a.shape[1:], a.dtype),
        compiler_params=params(),
    )(a, b)


def exchanged(values, orders, k, last, came, deps):
    out = []
    for p, order in enumerate(orders):
        before = list(deps)
        if came is not None:
            before += [came[q] for q in range(len(orders)) if orders[q][last] == order[k]]
        out.append(swapped(tied(values[p], *before) if before else values[p], order[k]))
    return out


def gather_round(held, came, orders, k, deps=()):
    if k > 0:
        held = [join(h, c) for h, c in zip(held, came)]
    return held, exchanged(held, orders, k, k - 1, came, deps)


def sum_cube(keep, send, orders, before):
    keep = [k.astype(f32) for k in keep]
    rounds = len(orders[0])
    came = first = None
    for k in range(rounds - 1, -1, -1):
        came = exchanged(send, orders, k, k + 1, came, before.get(rounds - 1 - k, ()))
        first = came if first is None else first
        total = [a + c.astype(f32) for a, c in zip(keep, came)]
        half = total[0].shape[0] // 2
        if k > 0:
            send = [t[half:].astype(bf16) for t in total]
            keep = [t[:half] for t in total]
    return [t[0].astype(bf16) for t in total], first


def block_place(order, r, z):
    place = 0
    for k, (axis, bit) in enumerate(order):
        on = z if axis == "section" else (r >> bit) & 1
        place = place + (on << k)
    return place


AHEAD = 8
GROUP = 4


def units_of(orders, half, slices, early):
    out = []
    for p, order in enumerate(orders):
        for r in range(slices):
            here = all(block_place(order, r, z) < half for z in range(2))
            if here == early:
                out.append((p, r))
    return out


class Stream:
    def __init__(self):
        self.copies = []

    def add(self, src, dst, sem):
        self.copies.append(pltpu.make_async_copy(src, dst, sem))
        return len(self.copies) - 1

    def begin(self):
        for copy in self.copies[:AHEAD]:
            copy.start()

    def arrived(self, group):
        for i in group:
            self.copies[i].wait()
            if i + AHEAD < len(self.copies):
                self.copies[i + AHEAD].start()


def packed(units, spans):
    starts = [0]
    for p, _ in units:
        starts.append(starts[-1] + spans[p][1] - spans[p][0])
    return starts


def weight_copies(stream, units, feats, mine, gate_ref, up_ref, in_w, sems):
    spans = in_cuts(feats)
    starts = packed(units, spans)
    places = []
    for which, src in enumerate((gate_ref, up_ref)):
        for u, (p, r) in enumerate(units):
            a, b = spans[p]
            row = pl.multiple_of((mine ^ r) * feats + a, 128)
            dst = in_w.at[which, starts[u] : starts[u + 1]]
            sem = sems.at[len(places)]
            places.append(stream.add(src.at[pl.ds(row, b - a)], dst, sem))
    return places


def scale_rows(units, block, gain_ref, scaled, spans, squares):
    for u, (p, r) in enumerate(units):
        a, b = spans[p]
        x = jnp.concatenate([block(p, r, 0), block(p, r, 1)], axis=0).astype(f32)
        scaled[u, :, : b - a] = (x * gain_ref[r, :, a:b]).astype(bf16)
        for c in range(0, b - a, 128):
            squares = squares + x[:, c : c + 128] * x[:, c : c + 128]
    return squares


def product(stream, places, which, units, spans, scaled, in_w, base, n, tile):
    total = base
    starts = packed(units, spans)
    first = which * len(units)
    for u, (p, r) in enumerate(units):
        a, b = spans[p]
        if n == 0 and u % GROUP == 0:
            stream.arrived(places[first + u : first + min(u + GROUP, len(units))])
        term = jnp.dot(
            scaled[u, :, : b - a],
            in_w[which, starts[u] : starts[u + 1], n : n + tile],
            preferred_element_type=f32,
        )
        total = term if total is None else total + term
    return total


def early_kernel(units, orders, feats, me, *refs):
    early = refs[:IN_PARTS]
    gain_ref, gate_ref, up_ref, gate_out, up_out, squares_out = refs[IN_PARTS : IN_PARTS + 6]
    scaled, in_w, sems = refs[IN_PARTS + 6 :]
    rows = early[0].shape[1]
    spans = in_cuts(feats)
    stream = Stream()
    places = weight_copies(stream, units, feats, me[0], gate_ref, up_ref, in_w, sems)
    stream.begin()

    def block(p, r, z):
        return early[p][block_place(orders[p], r, z)]

    squares = jnp.zeros((2 * rows, 128), f32)
    squares_out[...] = scale_rows(units, block, gain_ref, scaled, spans, squares)
    count = gate_out.shape[1]
    tile = min(512, count)
    for first, out in enumerate((gate_out, up_out)):
        for n in range(0, count, tile):
            out[:, n : n + tile] = product(
                stream, places, first, units, spans, scaled, in_w, None, n, tile
            )


def late_kernel(units, orders, sum_orders, out_spans, feats, me, *refs):
    early, late = refs[:IN_PARTS], refs[IN_PARTS : 2 * IN_PARTS]
    refs = refs[2 * IN_PARTS :]
    gain_ref, gate_in, up_in, squares_in, gate_ref, up_ref, down_ref = refs[:7]
    outs = refs[7 : 7 + 2 * OUT_PARTS]
    scaled, hidden, in_w, down_w, sems, down_sems = refs[7 + 2 * OUT_PARTS :]
    half, rows = late[0].shape[:2]
    slices = half
    mine = me[0]
    spans = in_cuts(feats)
    stream = Stream()
    places = weight_copies(stream, units, feats, mine, gate_ref, up_ref, in_w, sems)
    down_places = []
    work = [(p, r) for p in range(OUT_PARTS) for r in range(slices)]
    for p, r in work:
        a, b = out_spans[p]
        col = pl.multiple_of((mine ^ r) * feats + a, 128)
        src = down_ref.at[:, pl.ds(col, b - a)]
        dst = down_w.at[r, :, a:b]
        down_places.append(stream.add(src, dst, down_sems.at[len(down_places)]))
    stream.begin()

    def block(p, r, z):
        place = block_place(orders[p], r, z)
        return early[p][place] if place < half else late[p][place - half]

    squares = scale_rows(units, block, gain_ref, scaled, spans, squares_in[...])
    inv = lax.rsqrt(jnp.sum(squares, axis=1, keepdims=True) / D + norm_eps)
    count = hidden.shape[1]
    tile = min(512, count)
    for n in range(0, count, tile):
        cols = slice(n, n + tile)
        gate = inv * product(
            stream, places, 0, units, spans, scaled, in_w, gate_in[:, cols], n, tile
        )
        up = inv * product(
            stream, places, 1, units, spans, scaled, in_w, up_in[:, cols], n, tile
        )
        hidden[:, cols] = (gate / (1.0 + jnp.exp(-gate)) * up).astype(bf16)

    for i, (p, r) in enumerate(work):
        if i % GROUP == 0:
            stream.arrived(down_places[i : i + GROUP])
        a, b = out_spans[p]
        out = jnp.dot(hidden[...], down_w[r, :, a:b], preferred_element_type=f32).astype(bf16)
        for z in range(2):
            place = block_place(sum_orders[p], r, z)
            part = out[z * rows : (z + 1) * rows]
            outs[2 * p + place // half][place % half] = part


def expert_params():
    return pltpu.CompilerParams(vmem_limit_bytes=40 * 1024 * 1024)


def experts_early(me, early, gain_all, gate_w, up_w, orders):
    half, rows = early[0].shape[:2]
    feats = gain_all.shape[2]
    count = gate_w.shape[1]
    widest = max(b - a for a, b in in_cuts(feats))
    units = units_of(orders, half, half, True)
    vmem = pl.BlockSpec(memory_space=pltpu.VMEM)
    hbm = pl.BlockSpec(memory_space=pltpu.HBM)
    total = jax.ShapeDtypeStruct((2 * rows, count), f32)
    return pl.pallas_call(
        functools.partial(early_kernel, units, orders, feats),
        name="experts_early",
        out_shape=(total, total, jax.ShapeDtypeStruct((2 * rows, 128), f32)),
        in_specs=[pl.BlockSpec(memory_space=pltpu.SMEM)]
        + [vmem] * (IN_PARTS + 1)
        + [hbm] * 2,
        out_specs=[vmem] * 3,
        scratch_shapes=[
            pltpu.VMEM((len(units), 2 * rows, widest), bf16),
            pltpu.VMEM((2, packed(units, in_cuts(feats))[-1], count), bf16),
            pltpu.SemaphoreType.DMA((2 * len(units),)),
        ],
        compiler_params=expert_params(),
        cost_estimate=pl.CostEstimate(
            flops=2 * 2 * rows * D * count,
            bytes_accessed=2 * D * count,
            transcendentals=0,
        ),
    )(me, *early, gain_all, gate_w, up_w)


def experts_late(
    me, early, late, gain_all, sums, gate_w, up_w, down_w, orders, sum_orders, out_spans
):
    half, rows = late[0].shape[:2]
    feats = gain_all.shape[2]
    count = gate_w.shape[1]
    widest = max(b - a for a, b in in_cuts(feats))
    units = units_of(orders, half, half, False)
    vmem = pl.BlockSpec(memory_space=pltpu.VMEM)
    hbm = pl.BlockSpec(memory_space=pltpu.HBM)
    outs = pl.pallas_call(
        functools.partial(late_kernel, units, orders, sum_orders, out_spans, feats),
        name="experts_late",
        out_shape=[
            jax.ShapeDtypeStruct((half, rows, b - a), bf16)
            for a, b in out_spans
            for _ in range(2)
        ],
        in_specs=[pl.BlockSpec(memory_space=pltpu.SMEM)]
        + [vmem] * (2 * IN_PARTS + 4)
        + [hbm] * 3,
        out_specs=[vmem] * (2 * OUT_PARTS),
        scratch_shapes=[
            pltpu.VMEM((len(units), 2 * rows, widest), bf16),
            pltpu.VMEM((2 * rows, count), bf16),
            pltpu.VMEM((2, packed(units, in_cuts(feats))[-1], count), bf16),
            pltpu.VMEM((half, count, feats), bf16),
            pltpu.SemaphoreType.DMA((2 * len(units),)),
            pltpu.SemaphoreType.DMA((half * OUT_PARTS,)),
        ],
        compiler_params=expert_params(),
        cost_estimate=pl.CostEstimate(
            flops=2 * 2 * rows * D * count * 2,
            bytes_accessed=4 * D * count,
            transcendentals=2 * rows * count,
        ),
    )(me, *early, *late, gain_all, *sums, gate_w, up_w, down_w)
    return outs[0::2], outs[1::2]


def tensor_sum(stat):
    for b in range(lax.axis_size("tensor").bit_length() - 1):
        stat = stat + swapped(stat, ("tensor", b))
    return stat


def first_sums(stat, gain_row):
    rows, feats = stat.shape[1], gain_row.shape[1]
    lines = -(-feats // rows)
    gains = jnp.pad(gain_row[0], (0, lines * rows - feats)).reshape(lines, rows)
    steps = []
    for b in range(lax.axis_size("tensor").bit_length() - 1):
        count = 9 + gains.shape[0]
        parcel = jnp.concatenate([stat[:9], gains, jnp.zeros((-count % 8, rows), f32)])
        came = swapped(parcel, ("tensor", b))
        stat = stat[:9] + came[:9]
        gains = jnp.concatenate([gains, came[9:count]])
        steps.append(came)
    gains = gains.reshape(lax.axis_size("tensor"), 1, lines * rows)[:, :, :feats]
    return stat, gains, steps


def on_device(tokens, norm_gain, router, w_gate, w_up, w_down, expert_ids, lengths):
    sections = lax.axis_size("section")
    slices = lax.axis_size("tensor")
    section = lax.axis_index("section")
    core = lax.axis_index("expert").astype(jnp.int32)[None]
    me = lax.axis_index("tensor").astype(jnp.int32)[None]
    layer = section // 2
    rows, feats = tokens.shape
    across = ("expert", 0)

    gain_row = lax.dynamic_index_in_dim(norm_gain, layer, 0, keepdims=True)
    router_t = lax.dynamic_index_in_dim(router, layer, 0, keepdims=False).T
    ids_rows = jnp.transpose(expert_ids, (0, 2, 1)).reshape(4, rows)
    lens = jnp.concatenate(
        [
            lax.dynamic_index_in_dim(lengths, section, 0, keepdims=False),
            lax.dynamic_index_in_dim(lengths, (section - 2) % sections, 0, keepdims=False),
        ]
    )
    orders = sum_orders = out_orders(slices)
    rounds = len(orders[0])
    gate_w, up_w, down_w = w_gate[0, 0], w_up[0, 0], w_down[0, 0]
    pieces = []
    begin = 0
    for share in (6, 7, 12, 7):
        pieces.append(tokens[begin : begin + rows * share // 32])
        begin += rows * share // 32

    slots, own, other = prologue(core, lens, ids_rows, tokens)
    next_slots = ahead(slots, -2)
    blocks = lay(own, swapped(other, across))
    held, came = gather_round(blocks, None, orders, 0)
    stat = stats(tied(tokens, *blocks), gain_row, router_t)
    stat, gain_all, steps = first_sums(stat, gain_row)
    for k in range(1, rounds):
        deps = steps[:1] if k == 1 else [next_slots] if k == rounds - 1 else []
        held, came = gather_round(held, came, orders, k, deps)
    far = [ahead(tied(pieces[0], *held), 2)]
    sums = experts_early(me, held, gain_all, gate_w, up_w, orders)
    aux, base, mix = prepare(core, stat, ids_rows, slots, next_slots, tied(tokens, *held))
    far_aux = ahead(aux, 2)

    came = [tied(c, far[0], mix) for c in came]
    far.append(ahead(tied(pieces[1], *came), 2))
    keep, send = experts_late(
        me, held, came, gain_all, sums, gate_w, up_w, down_w, orders, sum_orders, cuts(feats, OUT_PARTS)
    )
    far.append(ahead(tied(pieces[2], *send), 2))
    summed, _ = sum_cube(keep, send, sum_orders, {0: [far[1]], rounds - 1: [far[2]]})

    mine = [s[:CAP] for s in summed]
    theirs = [swapped(s[CAP:], across) for s in summed]
    to_own, to_other, slab_own, slab_other = repick(mix, base, mine, theirs)
    blocks = lay(ahead(to_own, 2), ahead(to_other, 2, True))
    slab_own = ahead(tied(slab_own, *blocks), 2)
    held, came = gather_round(blocks, None, orders, 0)
    for k in range(1, rounds):
        held, came = gather_round(held, came, orders, k, [slab_own] if k == rounds - 1 else [])
    slab_other = ahead(tied(slab_other, *held), 2)
    sums = experts_early(me, held, gain_all, gate_w, up_w, orders)
    came = [tied(c, slab_other) for c in came]
    far.append(ahead(tied(pieces[3], *came), 2))
    keep, send = experts_late(
        me,
        held,
        came,
        gain_all,
        sums,
        gate_w,
        up_w,
        down_w,
        orders,
        sum_orders,
        cuts(feats, OUT_PARTS),
    )

    summed, first = sum_cube(keep, send, sum_orders, {0: [far[3]]})
    far_tokens = jnp.concatenate(far, axis=0)
    far_aux = tied(far_aux, *first)
    state, stat = between(far_tokens, far_aux, slab_own, slab_other, gain_row, router_t)
    stat = tensor_sum(stat)
    mine = [s[:CAP] for s in summed]
    theirs = [swapped(s[CAP:], across) for s in summed]
    return last(core, state, stat, ids_rows, slots, mine, theirs)


def solution(mesh):
    in_specs = (
        P(("section", "expert"), "tensor"),
        P(None, "tensor"),
        P(None, "tensor", None),
        P("section", "expert", None, "tensor"),
        P("section", "expert", None, "tensor"),
        P("section", "expert", "tensor", None),
        P(None, ("section", "expert"), None),
        P(None, "expert"),
    )
    out_specs = P(("section", "expert"), "tensor")
    return jax.shard_map(
        on_device, mesh=mesh, in_specs=in_specs, out_specs=out_specs, check_vma=False
    )
```

```python
import functools

import jax
import jax.numpy as jnp
from jax import lax
from jax.experimental import pallas as pl
from jax.experimental.pallas import tpu as pltpu
from jax.sharding import PartitionSpec as P

D = 6144
E = 8
EXP_WIN = 2
SEQ_LEN = 128
CAP = 64
IN_PARTS = 3
OUT_PARTS = 3

norm_eps = 1e-05
VMEM_BYTES = 10 * 1024 * 1024

bf16 = jnp.bfloat16
f32 = jnp.float32


def params():
    return pltpu.CompilerParams(vmem_limit_bytes=VMEM_BYTES)


def cuts(feats, parts):
    ends = [feats // 128 * p // parts * 128 for p in range(parts + 1)]
    return list(zip(ends[:-1], ends[1:]))


def in_cuts(feats):
    units = feats // 128
    first = max(1, units // 6)
    second = (units - first) // 2
    ends = [0, first * 128, (first + second) * 128, feats]
    return list(zip(ends[:-1], ends[1:]))


def swapped(x, dim):
    axis, bit = dim
    return lax.ppermute(x, axis, [(i, i ^ (1 << bit)) for i in range(lax.axis_size(axis))])


def ahead(x, by, cross=False):
    sections, cores = lax.axis_size("section"), lax.axis_size("expert")
    perm = []
    for s in range(sections):
        for c in range(cores):
            there = (s + by) % sections * cores + (c ^ 1 if cross else c)
            perm.append((s * cores + c, there))
    return lax.ppermute(x, ("section", "expert"), perm)


def nt(a, b):
    return lax.dot_general(a, b, (((1,), (1,)), ((), ())), preferred_element_type=f32)


def tn(a, b):
    return lax.dot_general(a, b, (((0,), (0,)), ((), ())), preferred_element_type=f32)


def one_hot_rows(slot_row):
    rows = slot_row.shape[1]
    places = lax.broadcasted_iota(jnp.int32, (CAP, rows), 0).astype(f32)
    return places == slot_row


def prologue_kernel(place_ref, lens, ids_ref, x_hbm, slots_ref, own_ref, other_ref, x_ref, sem):
    copy = pltpu.make_async_copy(x_hbm, x_ref, sem)
    copy.start()
    rows = ids_ref.shape[2]
    groups_len = rows // SEQ_LEN
    place = lax.broadcasted_iota(jnp.int32, (1, rows), 1)
    me = place_ref[0]
    named = []
    for step in range(2):
        limit = jnp.zeros((1, rows), jnp.int32)
        for q in range(groups_len):
            limit = jnp.where(place // SEQ_LEN == q, lens[place_ref[1 + step], q], limit)
        live = place % SEQ_LEN < limit
        first = ids_ref[step, 0:1, :]
        second = ids_ref[step, 1:2, :]
        for which in range(2):
            expert = me if which == 0 else 1 - me
            hit = ((first == expert) | (second == expert)) & live
            named.append(jnp.where(hit, 1.0, 0.0))
    named.append(jnp.zeros((4, rows), f32))
    named = jnp.concatenate(named, axis=0)
    r = lax.broadcasted_iota(jnp.int32, (rows, rows), 0)
    c = lax.broadcasted_iota(jnp.int32, (rows, rows), 1)
    before = jnp.where(r < c, 1.0, 0.0).astype(bf16)
    earlier = jnp.dot(named.astype(bf16), before, preferred_element_type=f32)
    slots = jnp.where((named > 0.5) & (earlier < CAP), earlier, -1.0)
    slots_ref[...] = slots
    table = jnp.concatenate(
        [one_hot_rows(slots[0:1]), one_hot_rows(slots[1:2])], axis=0
    )
    table = jnp.where(table, 1.0, 0.0).astype(bf16)
    copy.wait()
    for a, b in cuts(x_ref.shape[1], OUT_PARTS):
        got = jnp.dot(table, x_ref[:, a:b], preferred_element_type=f32).astype(bf16)
        own_ref[:, a:b] = got[:CAP]
        other_ref[:, a:b] = got[CAP:]


def prologue(place, lens, ids_rows, x):
    rows, feats = x.shape
    piece = jax.ShapeDtypeStruct((CAP, feats), bf16)
    return pl.pallas_call(
        prologue_kernel,
        name="prologue",
        out_shape=(jax.ShapeDtypeStruct((8, rows), f32), piece, piece),
        in_specs=[
            pl.BlockSpec(memory_space=pltpu.SMEM),
            pl.BlockSpec(memory_space=pltpu.SMEM),
            pl.BlockSpec(memory_space=pltpu.VMEM),
            pl.BlockSpec(memory_space=pltpu.HBM),
        ],
        scratch_shapes=[pltpu.VMEM((rows, feats), bf16), pltpu.SemaphoreType.DMA(())],
        compiler_params=params(),
    )(place, lens, ids_rows, x)


def in_three(v):
    first = v.astype(bf16)
    rest = v - first.astype(f32)
    second = rest.astype(bf16)
    return first, second, (rest - second.astype(f32)).astype(bf16)


def row_stats(x_bf, gain, router_t):
    parts = jnp.concatenate(in_three(router_t * gain), axis=0)
    got = nt(parts, x_bf)
    logits = (got[16:] + got[8:16]) + got[:8]
    xf = x_bf.astype(f32)
    squares = xf[:, :128] * xf[:, :128]
    for c in range(128, xf.shape[1], 128):
        squares = squares + xf[:, c : c + 128] * xf[:, c : c + 128]
    ones = jnp.ones((8, 128), bf16)
    first, second, third = in_three(squares)
    return logits, (nt(ones, third) + nt(ones, second)) + nt(ones, first)


def stats_kernel(x_ref, gain_ref, router_ref, out_ref):
    logits, sq = row_stats(x_ref[...], gain_ref[...], router_ref[...])
    out_ref[:8] = logits
    out_ref[8:] = sq


def stats(x, gain_row, router_t):
    return pl.pallas_call(
        stats_kernel,
        name="stats",
        out_shape=jax.ShapeDtypeStruct((16, x.shape[0]), f32),
        compiler_params=params(),
    )(x, gain_row, router_t)


def row_weights(stat, first, second, me):
    inv = lax.rsqrt(stat[8:9] / D + norm_eps)
    logits = stat[:8] * inv
    names = lax.broadcasted_iota(jnp.int32, logits.shape, 0)
    a = jnp.sum(jnp.where(names == first, logits, 0.0), axis=0, keepdims=True)
    b = jnp.sum(jnp.where(names == second, logits, 0.0), axis=0, keepdims=True)
    wa = jax.nn.sigmoid(a - b)
    wb = jax.nn.sigmoid(b - a)
    out = []
    for which in range(2):
        expert = me if which == 0 else 1 - me
        out.append(jnp.where(first == expert, wa, 0.0) + jnp.where(second == expert, wb, 0.0))
    return out


def weight_table(weights, slots):
    parts = []
    for w, slot in zip(weights, slots):
        hot = one_hot_rows(slot)
        hi = w.astype(bf16).astype(f32)
        lo = w - hi
        parts.append(jnp.where(hot, hi, 0.0).astype(bf16))
        parts.append(jnp.where(hot, lo, 0.0).astype(bf16))
    return jnp.concatenate(parts, axis=0)


def stacked(own, other):
    return jnp.concatenate([own, own, other, other], axis=0)


def prepare_kernel(core, stat_ref, ids_ref, slots_ref, next_ref, x_ref, aux_ref, base_ref, mix_ref):
    me = core[0]
    w_own, w_other = row_weights(stat_ref[...], ids_ref[0, 0:1, :], ids_ref[0, 1:2, :], me)
    s_own, s_other = slots_ref[0:1, :], slots_ref[1:2, :]
    aux_ref[...] = jnp.concatenate(
        [w_own, w_other, s_own, s_other, jnp.zeros((4, w_own.shape[1]), f32)], axis=0
    )
    table = weight_table((w_own, w_other), (s_own, s_other))
    pick = jnp.concatenate([one_hot_rows(next_ref[2:3, :]), one_hot_rows(next_ref[3:4, :])], axis=0)
    pick = jnp.where(pick, 1.0, 0.0).astype(bf16)
    mix_ref[...] = nt(pick, table).astype(bf16)
    for a, b in cuts(x_ref.shape[1], OUT_PARTS):
        got = jnp.dot(pick, x_ref[:, a:b], preferred_element_type=f32)
        base_ref[:, a:b] = got.astype(bf16)


def prepare(core, stat, ids_rows, slots, next_slots, x):
    rows, feats = x.shape
    vmem = pl.BlockSpec(memory_space=pltpu.VMEM)
    return pl.pallas_call(
        prepare_kernel,
        name="prepare",
        out_shape=(
            jax.ShapeDtypeStruct((8, rows), f32),
            jax.ShapeDtypeStruct((2 * CAP, feats), bf16),
            jax.ShapeDtypeStruct((2 * CAP, 4 * CAP), bf16),
        ),
        in_specs=[pl.BlockSpec(memory_space=pltpu.SMEM)] + [vmem] * 5,
        compiler_params=params(),
    )(core, stat, ids_rows, slots, next_slots, x)


def repick_kernel(mix_ref, base_ref, *refs):
    own, other = refs[:OUT_PARTS], refs[OUT_PARTS : 2 * OUT_PARTS]
    to_own_ref, to_other_ref, own_ref, other_ref = refs[2 * OUT_PARTS :]
    for p, (a, b) in enumerate(cuts(base_ref.shape[1], OUT_PARTS)):
        rows = jnp.dot(
            mix_ref[...], stacked(own[p][...], other[p][...]), preferred_element_type=f32
        )
        rows = (base_ref[:, a:b].astype(f32) + rows).astype(bf16)
        to_own_ref[:, a:b] = rows[:CAP]
        to_other_ref[:, a:b] = rows[CAP:]
        own_ref[:, a:b] = own[p][...]
        other_ref[:, a:b] = other[p][...]


def repick(mix, base, own, other):
    piece = jax.ShapeDtypeStruct((CAP, base.shape[1]), bf16)
    return pl.pallas_call(
        repick_kernel, name="repick", out_shape=(piece,) * 4, compiler_params=params()
    )(mix, base, *own, *other)


def lay_kernel(own_ref, other_ref, *outs):
    for out, (a, b) in zip(outs, in_cuts(own_ref.shape[1])):
        out[0, :CAP] = own_ref[:, a:b]
        out[0, CAP:] = other_ref[:, a:b]


def lay(own, other):
    return pl.pallas_call(
        lay_kernel,
        name="lay",
        out_shape=[
            jax.ShapeDtypeStruct((1, 2 * CAP, b - a), bf16)
            for a, b in in_cuts(own.shape[1])
        ],
        compiler_params=params(),
    )(own, other)


def between_kernel(x_ref, aux_ref, own_ref, other_ref, gain_ref, router_ref, new_ref, stat_ref):
    table = weight_table((aux_ref[0:1, :], aux_ref[1:2, :]), (aux_ref[2:3, :], aux_ref[3:4, :]))
    logits = None
    for a, b in cuts(x_ref.shape[1], OUT_PARTS):
        cols = slice(a, b)
        mixed = tn(table, stacked(own_ref[:, cols], other_ref[:, cols]))
        new = (x_ref[:, cols].astype(f32) + mixed).astype(bf16)
        new_ref[:, cols] = new
        l, s = row_stats(new, gain_ref[:, cols], router_ref[:, cols])
        logits = l if logits is None else logits + l
        sq = s if a == 0 else sq + s
    stat_ref[:8] = logits
    stat_ref[8:] = sq


def between(x, aux, own, other, gain_row, router_t):
    return pl.pallas_call(
        between_kernel,
        name="between",
        out_shape=(
            jax.ShapeDtypeStruct(x.shape, bf16),
            jax.ShapeDtypeStruct((16, x.shape[0]), f32),
        ),
        compiler_params=params(),
    )(x, aux, own, other, gain_row, router_t)


def last_kernel(core, x_ref, stat_ref, ids_ref, slots_ref, *refs):
    own, other, out_ref = refs[:OUT_PARTS], refs[OUT_PARTS : 2 * OUT_PARTS], refs[-1]
    me = core[0]
    weights = row_weights(stat_ref[...], ids_ref[1, 0:1, :], ids_ref[1, 1:2, :], me)
    table = weight_table(weights, (slots_ref[2:3, :], slots_ref[3:4, :]))
    for p, (a, b) in enumerate(cuts(x_ref.shape[1], OUT_PARTS)):
        cols = slice(a, b)
        mixed = tn(table, stacked(own[p][...], other[p][...]))
        out_ref[:, cols] = (x_ref[:, cols].astype(f32) + mixed).astype(bf16)


def last(core, x, stat, ids_rows, slots, own, other):
    vmem = pl.BlockSpec(memory_space=pltpu.VMEM)
    return pl.pallas_call(
        last_kernel,
        name="last",
        out_shape=jax.ShapeDtypeStruct(x.shape, bf16),
        in_specs=[pl.BlockSpec(memory_space=pltpu.SMEM)] + [vmem] * (4 + 2 * OUT_PARTS),
        compiler_params=params(),
    )(core, x, stat, ids_rows, slots, *own, *other)


def out_orders(slices):
    bits = slices.bit_length() - 1
    dims = [("tensor", b) for b in range(bits)] + [("section", 0)]
    n = len(dims)
    return [[dims[(i + p * max(1, n // OUT_PARTS)) % n] for i in range(n)] for p in range(OUT_PARTS)]


def tied(x, *before):
    return lax.optimization_barrier((x, before))[0]


def join_kernel(a_ref, b_ref, out_ref):
    half = a_ref.shape[0]
    out_ref[:half] = a_ref[...]
    out_ref[half:] = b_ref[...]


def join(a, b):
    return pl.pallas_call(
        join_kernel,
        name="join",
        out_shape=jax.ShapeDtypeStruct((2 * a.shape[0],) + a.shape[1:], a.dtype),
        compiler_params=params(),
    )(a, b)


def exchanged(values, orders, k, last, came, deps):
    out = []
    for p, order in enumerate(orders):
        before = list(deps)
        if came is not None:
            before += [came[q] for q in range(len(orders)) if orders[q][last] == order[k]]
        out.append(swapped(tied(values[p], *before) if before else values[p], order[k]))
    return out


def gather_round(held, came, orders, k, deps=()):
    if k > 0:
        held = [join(h, c) for h, c in zip(held, came)]
    return held, exchanged(held, orders, k, k - 1, came, deps)


def sum_cube(keep, send, orders, before):
    keep = [k.astype(f32) for k in keep]
    rounds = len(orders[0])
    came = first = None
    for k in range(rounds - 1, -1, -1):
        came = exchanged(send, orders, k, k + 1, came, before.get(rounds - 1 - k, ()))
        first = came if first is None else first
        total = [a + c.astype(f32) for a, c in zip(keep, came)]
        half = total[0].shape[0] // 2
        if k > 0:
            send = [t[half:].astype(bf16) for t in total]
            keep = [t[:half] for t in total]
    return [t[0].astype(bf16) for t in total], first


def block_place(order, r, z):
    place = 0
    for k, (axis, bit) in enumerate(order):
        on = z if axis == "section" else (r >> bit) & 1
        place = place + (on << k)
    return place


AHEAD = 8
GROUP = 4


def units_of(orders, half, slices, early):
    out = []
    for p, order in enumerate(orders):
        for r in range(slices):
            here = all(block_place(order, r, z) < half for z in range(2))
            if here == early:
                out.append((p, r))
    return out


class Stream:
    def __init__(self):
        self.copies = []

    def add(self, src, dst, sem):
        self.copies.append(pltpu.make_async_copy(src, dst, sem))
        return len(self.copies) - 1

    def begin(self):
        for copy in self.copies[:AHEAD]:
            copy.start()

    def arrived(self, group):
        for i in group:
            self.copies[i].wait()
            if i + AHEAD < len(self.copies):
                self.copies[i + AHEAD].start()


def packed(units, spans):
    starts = [0]
    for p, _ in units:
        starts.append(starts[-1] + spans[p][1] - spans[p][0])
    return starts


def weight_copies(stream, units, feats, mine, gate_ref, up_ref, in_w, sems):
    spans = in_cuts(feats)
    starts = packed(units, spans)
    places = []
    for which, src in enumerate((gate_ref, up_ref)):
        for u, (p, r) in enumerate(units):
            a, b = spans[p]
            row = pl.multiple_of((mine ^ r) * feats + a, 128)
            dst = in_w.at[which, starts[u] : starts[u + 1]]
            sem = sems.at[len(places)]
            places.append(stream.add(src.at[pl.ds(row, b - a)], dst, sem))
    return places


def scale_rows(units, block, gain_ref, scaled, spans, squares):
    for u, (p, r) in enumerate(units):
        a, b = spans[p]
        x = jnp.concatenate([block(p, r, 0), block(p, r, 1)], axis=0).astype(f32)
        scaled[u, :, : b - a] = (x * gain_ref[r, :, a:b]).astype(bf16)
        for c in range(0, b - a, 128):
            squares = squares + x[:, c : c + 128] * x[:, c : c + 128]
    return squares


def product(stream, places, which, units, spans, scaled, in_w, base, n, tile):
    total = base
    starts = packed(units, spans)
    first = which * len(units)
    for u, (p, r) in enumerate(units):
        a, b = spans[p]
        if n == 0 and u % GROUP == 0:
            stream.arrived(places[first + u : first + min(u + GROUP, len(units))])
        term = jnp.dot(
            scaled[u, :, : b - a],
            in_w[which, starts[u] : starts[u + 1], n : n + tile],
            preferred_element_type=f32,
        )
        total = term if total is None else total + term
    return total


def early_kernel(units, orders, feats, me, *refs):
    early = refs[:IN_PARTS]
    gain_ref, gate_ref, up_ref, gate_out, up_out, squares_out = refs[IN_PARTS : IN_PARTS + 6]
    scaled, in_w, sems = refs[IN_PARTS + 6 :]
    rows = early[0].shape[1]
    spans = in_cuts(feats)
    stream = Stream()
    places = weight_copies(stream, units, feats, me[0], gate_ref, up_ref, in_w, sems)
    stream.begin()

    def block(p, r, z):
        return early[p][block_place(orders[p], r, z)]

    squares = jnp.zeros((2 * rows, 128), f32)
    squares_out[...] = scale_rows(units, block, gain_ref, scaled, spans, squares)
    count = gate_out.shape[1]
    tile = min(512, count)
    for first, out in enumerate((gate_out, up_out)):
        for n in range(0, count, tile):
            out[:, n : n + tile] = product(
                stream, places, first, units, spans, scaled, in_w, None, n, tile
            )


def late_kernel(units, orders, sum_orders, out_spans, feats, me, *refs):
    early, late = refs[:IN_PARTS], refs[IN_PARTS : 2 * IN_PARTS]
    refs = refs[2 * IN_PARTS :]
    gain_ref, gate_in, up_in, squares_in, gate_ref, up_ref, down_ref = refs[:7]
    outs = refs[7 : 7 + 2 * OUT_PARTS]
    scaled, hidden, in_w, down_w, sems, down_sems = refs[7 + 2 * OUT_PARTS :]
    half, rows = late[0].shape[:2]
    slices = half
    mine = me[0]
    spans = in_cuts(feats)
    stream = Stream()
    places = weight_copies(stream, units, feats, mine, gate_ref, up_ref, in_w, sems)
    down_places = []
    work = [(p, r) for p in range(OUT_PARTS) for r in range(slices)]
    for p, r in work:
        a, b = out_spans[p]
        col = pl.multiple_of((mine ^ r) * feats + a, 128)
        src = down_ref.at[:, pl.ds(col, b - a)]
        dst = down_w.at[r, :, a:b]
        down_places.append(stream.add(src, dst, down_sems.at[len(down_places)]))
    stream.begin()

    def block(p, r, z):
        place = block_place(orders[p], r, z)
        return early[p][place] if place < half else late[p][place - half]

    squares = scale_rows(units, block, gain_ref, scaled, spans, squares_in[...])
    inv = lax.rsqrt(jnp.sum(squares, axis=1, keepdims=True) / D + norm_eps)
    count = hidden.shape[1]
    tile = min(512, count)
    for n in range(0, count, tile):
        cols = slice(n, n + tile)
        gate = inv * product(
            stream, places, 0, units, spans, scaled, in_w, gate_in[:, cols], n, tile
        )
        up = inv * product(
            stream, places, 1, units, spans, scaled, in_w, up_in[:, cols], n, tile
        )
        hidden[:, cols] = (gate / (1.0 + jnp.exp(-gate)) * up).astype(bf16)

    for i, (p, r) in enumerate(work):
        if i % GROUP == 0:
            stream.arrived(down_places[i : i + GROUP])
        a, b = out_spans[p]
        out = jnp.dot(hidden[...], down_w[r, :, a:b], preferred_element_type=f32).astype(bf16)
        for z in range(2):
            place = block_place(sum_orders[p], r, z)
            part = out[z * rows : (z + 1) * rows]
            outs[2 * p + place // half][place % half] = part


def expert_params():
    return pltpu.CompilerParams(vmem_limit_bytes=40 * 1024 * 1024)


def experts_early(me, early, gain_all, gate_w, up_w, orders):
    half, rows = early[0].shape[:2]
    feats = gain_all.shape[2]
    count = gate_w.shape[1]
    widest = max(b - a for a, b in in_cuts(feats))
    units = units_of(orders, half, half, True)
    vmem = pl.BlockSpec(memory_space=pltpu.VMEM)
    hbm = pl.BlockSpec(memory_space=pltpu.HBM)
    total = jax.ShapeDtypeStruct((2 * rows, count), f32)
    return pl.pallas_call(
        functools.partial(early_kernel, units, orders, feats),
        name="experts_early",
        out_shape=(total, total, jax.ShapeDtypeStruct((2 * rows, 128), f32)),
        in_specs=[pl.BlockSpec(memory_space=pltpu.SMEM)]
        + [vmem] * (IN_PARTS + 1)
        + [hbm] * 2,
        out_specs=[vmem] * 3,
        scratch_shapes=[
            pltpu.VMEM((len(units), 2 * rows, widest), bf16),
            pltpu.VMEM((2, packed(units, in_cuts(feats))[-1], count), bf16),
            pltpu.SemaphoreType.DMA((2 * len(units),)),
        ],
        compiler_params=expert_params(),
        cost_estimate=pl.CostEstimate(
            flops=2 * 2 * rows * D * count,
            bytes_accessed=2 * D * count,
            transcendentals=0,
        ),
    )(me, *early, gain_all, gate_w, up_w)


def experts_late(
    me, early, late, gain_all, sums, gate_w, up_w, down_w, orders, sum_orders, out_spans
):
    half, rows = late[0].shape[:2]
    feats = gain_all.shape[2]
    count = gate_w.shape[1]
    widest = max(b - a for a, b in in_cuts(feats))
    units = units_of(orders, half, half, False)
    vmem = pl.BlockSpec(memory_space=pltpu.VMEM)
    hbm = pl.BlockSpec(memory_space=pltpu.HBM)
    outs = pl.pallas_call(
        functools.partial(late_kernel, units, orders, sum_orders, out_spans, feats),
        name="experts_late",
        out_shape=[
            jax.ShapeDtypeStruct((half, rows, b - a), bf16)
            for a, b in out_spans
            for _ in range(2)
        ],
        in_specs=[pl.BlockSpec(memory_space=pltpu.SMEM)]
        + [vmem] * (2 * IN_PARTS + 4)
        + [hbm] * 3,
        out_specs=[vmem] * (2 * OUT_PARTS),
        scratch_shapes=[
            pltpu.VMEM((len(units), 2 * rows, widest), bf16),
            pltpu.VMEM((2 * rows, count), bf16),
            pltpu.VMEM((2, packed(units, in_cuts(feats))[-1], count), bf16),
            pltpu.VMEM((half, count, feats), bf16),
            pltpu.SemaphoreType.DMA((2 * len(units),)),
            pltpu.SemaphoreType.DMA((half * OUT_PARTS,)),
        ],
        compiler_params=expert_params(),
        cost_estimate=pl.CostEstimate(
            flops=2 * 2 * rows * D * count * 2,
            bytes_accessed=4 * D * count,
            transcendentals=2 * rows * count,
        ),
    )(me, *early, *late, gain_all, *sums, gate_w, up_w, down_w)
    return outs[0::2], outs[1::2]


def tensor_sum(stat):
    for b in range(lax.axis_size("tensor").bit_length() - 1):
        stat = stat + swapped(stat, ("tensor", b))
    return stat


def first_sums(stat, gain_row):
    rows, feats = stat.shape[1], gain_row.shape[1]
    lines = -(-feats // rows)
    gains = jnp.pad(gain_row[0], (0, lines * rows - feats)).reshape(lines, rows)
    steps = []
    for b in range(lax.axis_size("tensor").bit_length() - 1):
        count = 9 + gains.shape[0]
        parcel = jnp.concatenate([stat[:9], gains, jnp.zeros((-count % 8, rows), f32)])
        came = swapped(parcel, ("tensor", b))
        stat = stat[:9] + came[:9]
        gains = jnp.concatenate([gains, came[9:count]])
        steps.append(came)
    gains = gains.reshape(lax.axis_size("tensor"), 1, lines * rows)[:, :, :feats]
    return stat, gains, steps


def on_device(tokens, norm_gain, router, w_gate, w_up, w_down, expert_ids, lengths):
    sections = lax.axis_size("section")
    slices = lax.axis_size("tensor")
    section = lax.axis_index("section")
    core = lax.axis_index("expert").astype(jnp.int32)[None]
    me = lax.axis_index("tensor").astype(jnp.int32)[None]
    layer = section // 2
    rows, feats = tokens.shape
    across = ("expert", 0)

    gain_row = lax.dynamic_index_in_dim(norm_gain, layer, 0, keepdims=True)
    router_t = lax.dynamic_index_in_dim(router, layer, 0, keepdims=False).T
    ids_rows = jnp.transpose(expert_ids, (0, 2, 1))
    place = jnp.stack([core[0], section, (section - 2) % sections]).astype(jnp.int32)
    orders = sum_orders = out_orders(slices)
    rounds = len(orders[0])
    gate_w, up_w, down_w = w_gate[0, 0], w_up[0, 0], w_down[0, 0]
    pieces = []
    begin = 0
    for share in (5, 7, 13, 7):
        pieces.append(tokens[begin : begin + rows * share // 32])
        begin += rows * share // 32

    slots, own, other = prologue(place, lengths, ids_rows, tokens)
    next_slots = ahead(slots, -2)
    blocks = lay(own, swapped(other, across))
    held, came = gather_round(blocks, None, orders, 0)
    stat = stats(tied(tokens, *blocks), gain_row, router_t)
    stat, gain_all, steps = first_sums(stat, gain_row)
    for k in range(1, rounds):
        deps = steps[:1] if k == 1 else [next_slots] if k == rounds - 1 else []
        held, came = gather_round(held, came, orders, k, deps)
    far = [ahead(tied(pieces[0], *held), 2)]
    sums = experts_early(me, held, gain_all, gate_w, up_w, orders)
    aux, base, mix = prepare(core, stat, ids_rows, slots, next_slots, tied(tokens, *held))
    far_aux = ahead(aux, 2)

    came = [tied(c, far[0], mix) for c in came]
    far.append(ahead(tied(pieces[1], *came), 2))
    keep, send = experts_late(
        me, held, came, gain_all, sums, gate_w, up_w, down_w, orders, sum_orders, cuts(feats, OUT_PARTS)
    )
    far.append(ahead(tied(pieces[2], *send), 2))
    summed, _ = sum_cube(keep, send, sum_orders, {0: [far[1]]})

    mine = [s[:CAP] for s in summed]
    theirs = [swapped(s[CAP:], across) for s in summed]
    to_own, to_other, slab_own, slab_other = repick(mix, base, mine, theirs)
    to_own, to_other = tied(to_own, far[2]), tied(to_other, far[2])
    blocks = lay(ahead(to_own, 2), ahead(to_other, 2, True))
    slab_own = ahead(tied(slab_own, *blocks), 2)
    held, came = gather_round(blocks, None, orders, 0)
    for k in range(1, rounds):
        held, came = gather_round(held, came, orders, k, [slab_own] if k == rounds - 1 else [])
    slab_other = ahead(tied(slab_other, *held), 2)
    sums = experts_early(me, held, gain_all, gate_w, up_w, orders)
    came = [tied(c, slab_other) for c in came]
    far.append(ahead(tied(pieces[3], *came), 2))
    keep, send = experts_late(
        me,
        held,
        came,
        gain_all,
        sums,
        gate_w,
        up_w,
        down_w,
        orders,
        sum_orders,
        cuts(feats, OUT_PARTS),
    )

    summed, first = sum_cube(keep, send, sum_orders, {0: [far[3]]})
    far_tokens = jnp.concatenate(far, axis=0)
    far_aux = tied(far_aux, *first)
    state, stat = between(far_tokens, far_aux, slab_own, slab_other, gain_row, router_t)
    stat = tensor_sum(stat)
    mine = [s[:CAP] for s in summed]
    theirs = [swapped(s[CAP:], across) for s in summed]
    return last(core, state, stat, ids_rows, slots, mine, theirs)


def solution(mesh):
    in_specs = (
        P(("section", "expert"), "tensor"),
        P(None, "tensor"),
        P(None, "tensor", None),
        P("section", "expert", None, "tensor"),
        P("section", "expert", None, "tensor"),
        P("section", "expert", "tensor", None),
        P(None, ("section", "expert"), None),
        P(None, "expert"),
    )
    out_specs = P(("section", "expert"), "tensor")
    return jax.shard_map(
        on_device, mesh=mesh, in_specs=in_specs, out_specs=out_specs, check_vma=False
    )
```

```python
import functools

import jax
import jax.numpy as jnp
from jax import lax
from jax.experimental import pallas as pl
from jax.experimental.pallas import tpu as pltpu
from jax.sharding import PartitionSpec as P

D = 6144
E = 8
EXP_WIN = 2
SEQ_LEN = 128
CAP = 64
IN_PARTS = 3
OUT_PARTS = 3

norm_eps = 1e-05
VMEM_BYTES = 10 * 1024 * 1024

bf16 = jnp.bfloat16
f32 = jnp.float32


def params():
    return pltpu.CompilerParams(vmem_limit_bytes=VMEM_BYTES)


def cuts(feats, parts):
    ends = [feats // 128 * p // parts * 128 for p in range(parts + 1)]
    return list(zip(ends[:-1], ends[1:]))


def in_cuts(feats):
    units = feats // 128
    first = max(1, units // 6)
    second = (units - first) // 2
    ends = [0, first * 128, (first + second) * 128, feats]
    return list(zip(ends[:-1], ends[1:]))


def swapped(x, dim):
    axis, bit = dim
    return lax.ppermute(x, axis, [(i, i ^ (1 << bit)) for i in range(lax.axis_size(axis))])


def ahead(x, by, cross=False):
    sections, cores = lax.axis_size("section"), lax.axis_size("expert")
    perm = []
    for s in range(sections):
        for c in range(cores):
            there = (s + by) % sections * cores + (c ^ 1 if cross else c)
            perm.append((s * cores + c, there))
    return lax.ppermute(x, ("section", "expert"), perm)


def nt(a, b):
    return lax.dot_general(a, b, (((1,), (1,)), ((), ())), preferred_element_type=f32)


def tn(a, b):
    return lax.dot_general(a, b, (((0,), (0,)), ((), ())), preferred_element_type=f32)


def one_hot_rows(slot_row):
    rows = slot_row.shape[1]
    places = lax.broadcasted_iota(jnp.int32, (CAP, rows), 0).astype(f32)
    return places == slot_row


def prologue_kernel(place_ref, lens, ids_ref, x_hbm, slots_ref, own_ref, other_ref, x_ref, sem):
    copy = pltpu.make_async_copy(x_hbm, x_ref, sem)
    copy.start()
    rows = ids_ref.shape[2]
    groups_len = rows // SEQ_LEN
    place = lax.broadcasted_iota(jnp.int32, (1, rows), 1)
    me = place_ref[0]
    named = []
    for step in range(2):
        limit = jnp.zeros((1, rows), jnp.int32)
        for q in range(groups_len):
            limit = jnp.where(place // SEQ_LEN == q, lens[place_ref[1 + step], q], limit)
        live = place % SEQ_LEN < limit
        first = ids_ref[step, 0:1, :]
        second = ids_ref[step, 1:2, :]
        for which in range(2):
            expert = me if which == 0 else 1 - me
            hit = ((first == expert) | (second == expert)) & live
            named.append(jnp.where(hit, 1.0, 0.0))
    named.append(jnp.zeros((4, rows), f32))
    named = jnp.concatenate(named, axis=0)
    r = lax.broadcasted_iota(jnp.int32, (rows, rows), 0)
    c = lax.broadcasted_iota(jnp.int32, (rows, rows), 1)
    before = jnp.where(r < c, 1.0, 0.0).astype(bf16)
    earlier = jnp.dot(named.astype(bf16), before, preferred_element_type=f32)
    slots = jnp.where((named > 0.5) & (earlier < CAP), earlier, -1.0)
    slots_ref[...] = slots
    table = jnp.concatenate(
        [one_hot_rows(slots[0:1]), one_hot_rows(slots[1:2])], axis=0
    )
    table = jnp.where(table, 1.0, 0.0).astype(bf16)
    copy.wait()
    for a, b in cuts(x_ref.shape[1], OUT_PARTS):
        got = jnp.dot(table, x_ref[:, a:b], preferred_element_type=f32).astype(bf16)
        own_ref[:, a:b] = got[:CAP]
        other_ref[:, a:b] = got[CAP:]


def prologue(place, lens, ids_rows, x):
    rows, feats = x.shape
    piece = jax.ShapeDtypeStruct((CAP, feats), bf16)
    return pl.pallas_call(
        prologue_kernel,
        name="prologue",
        out_shape=(jax.ShapeDtypeStruct((8, rows), f32), piece, piece),
        in_specs=[
            pl.BlockSpec(memory_space=pltpu.SMEM),
            pl.BlockSpec(memory_space=pltpu.SMEM),
            pl.BlockSpec(memory_space=pltpu.VMEM),
            pl.BlockSpec(memory_space=pltpu.HBM),
        ],
        scratch_shapes=[pltpu.VMEM((rows, feats), bf16), pltpu.SemaphoreType.DMA(())],
        compiler_params=params(),
    )(place, lens, ids_rows, x)


def in_three(v):
    first = v.astype(bf16)
    rest = v - first.astype(f32)
    second = rest.astype(bf16)
    return first, second, (rest - second.astype(f32)).astype(bf16)


def row_stats(x_bf, gain, router_t):
    parts = jnp.concatenate(in_three(router_t * gain), axis=0)
    got = nt(parts, x_bf)
    logits = (got[16:] + got[8:16]) + got[:8]
    xf = x_bf.astype(f32)
    squares = xf[:, :128] * xf[:, :128]
    for c in range(128, xf.shape[1], 128):
        squares = squares + xf[:, c : c + 128] * xf[:, c : c + 128]
    ones = jnp.ones((8, 128), bf16)
    first, second, third = in_three(squares)
    return logits, (nt(ones, third) + nt(ones, second)) + nt(ones, first)


def stats_kernel(x_ref, gain_ref, router_ref, out_ref):
    logits, sq = row_stats(x_ref[...], gain_ref[...], router_ref[...])
    out_ref[:8] = logits
    out_ref[8:] = sq


def stats(x, gain_row, router_t):
    return pl.pallas_call(
        stats_kernel,
        name="stats",
        out_shape=jax.ShapeDtypeStruct((16, x.shape[0]), f32),
        compiler_params=params(),
    )(x, gain_row, router_t)


def row_weights(stat, first, second, me):
    inv = lax.rsqrt(stat[8:9] / D + norm_eps)
    logits = stat[:8] * inv
    names = lax.broadcasted_iota(jnp.int32, logits.shape, 0)
    a = jnp.sum(jnp.where(names == first, logits, 0.0), axis=0, keepdims=True)
    b = jnp.sum(jnp.where(names == second, logits, 0.0), axis=0, keepdims=True)
    wa = jax.nn.sigmoid(a - b)
    wb = jax.nn.sigmoid(b - a)
    out = []
    for which in range(2):
        expert = me if which == 0 else 1 - me
        out.append(jnp.where(first == expert, wa, 0.0) + jnp.where(second == expert, wb, 0.0))
    return out


def weight_table(weights, slots):
    parts = []
    for w, slot in zip(weights, slots):
        hot = one_hot_rows(slot)
        hi = w.astype(bf16).astype(f32)
        lo = w - hi
        parts.append(jnp.where(hot, hi, 0.0).astype(bf16))
        parts.append(jnp.where(hot, lo, 0.0).astype(bf16))
    return jnp.concatenate(parts, axis=0)


def stacked(own, other):
    return jnp.concatenate([own, own, other, other], axis=0)


def prepare_kernel(core, stat_ref, ids_ref, slots_ref, next_ref, x_ref, aux_ref, base_ref, mix_ref):
    me = core[0]
    w_own, w_other = row_weights(stat_ref[...], ids_ref[0, 0:1, :], ids_ref[0, 1:2, :], me)
    s_own, s_other = slots_ref[0:1, :], slots_ref[1:2, :]
    aux_ref[...] = jnp.concatenate(
        [w_own, w_other, s_own, s_other, jnp.zeros((4, w_own.shape[1]), f32)], axis=0
    )
    table = weight_table((w_own, w_other), (s_own, s_other))
    pick = jnp.concatenate([one_hot_rows(next_ref[2:3, :]), one_hot_rows(next_ref[3:4, :])], axis=0)
    pick = jnp.where(pick, 1.0, 0.0).astype(bf16)
    mix_ref[...] = nt(pick, table).astype(bf16)
    for a, b in cuts(x_ref.shape[1], OUT_PARTS):
        got = jnp.dot(pick, x_ref[:, a:b], preferred_element_type=f32)
        base_ref[:, a:b] = got.astype(bf16)


def prepare(core, stat, ids_rows, slots, next_slots, x):
    rows, feats = x.shape
    vmem = pl.BlockSpec(memory_space=pltpu.VMEM)
    return pl.pallas_call(
        prepare_kernel,
        name="prepare",
        out_shape=(
            jax.ShapeDtypeStruct((8, rows), f32),
            jax.ShapeDtypeStruct((2 * CAP, feats), bf16),
            jax.ShapeDtypeStruct((2 * CAP, 4 * CAP), bf16),
        ),
        in_specs=[pl.BlockSpec(memory_space=pltpu.SMEM)] + [vmem] * 5,
        compiler_params=params(),
    )(core, stat, ids_rows, slots, next_slots, x)


def repick_kernel(mix_ref, base_ref, *refs):
    own, other = refs[:OUT_PARTS], refs[OUT_PARTS : 2 * OUT_PARTS]
    to_own_ref, to_other_ref, own_ref, other_ref = refs[2 * OUT_PARTS :]
    for p, (a, b) in enumerate(cuts(base_ref.shape[1], OUT_PARTS)):
        rows = jnp.dot(
            mix_ref[...], stacked(own[p][...], other[p][...]), preferred_element_type=f32
        )
        rows = (base_ref[:, a:b].astype(f32) + rows).astype(bf16)
        to_own_ref[:, a:b] = rows[:CAP]
        to_other_ref[:, a:b] = rows[CAP:]
        own_ref[:, a:b] = own[p][...]
        other_ref[:, a:b] = other[p][...]


def repick(mix, base, own, other):
    piece = jax.ShapeDtypeStruct((CAP, base.shape[1]), bf16)
    return pl.pallas_call(
        repick_kernel, name="repick", out_shape=(piece,) * 4, compiler_params=params()
    )(mix, base, *own, *other)


def lay_kernel(own_ref, other_ref, *outs):
    for out, (a, b) in zip(outs, in_cuts(own_ref.shape[1])):
        out[0, :CAP] = own_ref[:, a:b]
        out[0, CAP:] = other_ref[:, a:b]


def lay(own, other):
    return pl.pallas_call(
        lay_kernel,
        name="lay",
        out_shape=[
            jax.ShapeDtypeStruct((1, 2 * CAP, b - a), bf16)
            for a, b in in_cuts(own.shape[1])
        ],
        compiler_params=params(),
    )(own, other)


def between_kernel(x_ref, aux_ref, own_ref, other_ref, gain_ref, router_ref, new_ref, stat_ref):
    table = weight_table((aux_ref[0:1, :], aux_ref[1:2, :]), (aux_ref[2:3, :], aux_ref[3:4, :]))
    logits = None
    for a, b in cuts(x_ref.shape[1], OUT_PARTS):
        cols = slice(a, b)
        mixed = tn(table, stacked(own_ref[:, cols], other_ref[:, cols]))
        new = (x_ref[:, cols].astype(f32) + mixed).astype(bf16)
        new_ref[:, cols] = new
        l, s = row_stats(new, gain_ref[:, cols], router_ref[:, cols])
        logits = l if logits is None else logits + l
        sq = s if a == 0 else sq + s
    stat_ref[:8] = logits
    stat_ref[8:] = sq


def between(x, aux, own, other, gain_row, router_t):
    return pl.pallas_call(
        between_kernel,
        name="between",
        out_shape=(
            jax.ShapeDtypeStruct(x.shape, bf16),
            jax.ShapeDtypeStruct((16, x.shape[0]), f32),
        ),
        compiler_params=params(),
    )(x, aux, own, other, gain_row, router_t)


def last_kernel(core, x_ref, stat_ref, ids_ref, slots_ref, *refs):
    own, other, out_ref = refs[:OUT_PARTS], refs[OUT_PARTS : 2 * OUT_PARTS], refs[-1]
    me = core[0]
    weights = row_weights(stat_ref[...], ids_ref[1, 0:1, :], ids_ref[1, 1:2, :], me)
    table = weight_table(weights, (slots_ref[2:3, :], slots_ref[3:4, :]))
    for p, (a, b) in enumerate(cuts(x_ref.shape[1], OUT_PARTS)):
        cols = slice(a, b)
        mixed = tn(table, stacked(own[p][...], other[p][...]))
        out_ref[:, cols] = (x_ref[:, cols].astype(f32) + mixed).astype(bf16)


def last(core, x, stat, ids_rows, slots, own, other):
    vmem = pl.BlockSpec(memory_space=pltpu.VMEM)
    return pl.pallas_call(
        last_kernel,
        name="last",
        out_shape=jax.ShapeDtypeStruct(x.shape, bf16),
        in_specs=[pl.BlockSpec(memory_space=pltpu.SMEM)] + [vmem] * (4 + 2 * OUT_PARTS),
        compiler_params=params(),
    )(core, x, stat, ids_rows, slots, *own, *other)


def out_orders(slices):
    bits = slices.bit_length() - 1
    dims = [("tensor", b) for b in range(bits)] + [("section", 0)]
    n = len(dims)
    return [[dims[(i + p * max(1, n // OUT_PARTS)) % n] for i in range(n)] for p in range(OUT_PARTS)]


def tied(x, *before):
    return lax.optimization_barrier((x, before))[0]


def join_kernel(a_ref, b_ref, out_ref):
    half = a_ref.shape[0]
    out_ref[:half] = a_ref[...]
    out_ref[half:] = b_ref[...]


def join(a, b):
    return pl.pallas_call(
        join_kernel,
        name="join",
        out_shape=jax.ShapeDtypeStruct((2 * a.shape[0],) + a.shape[1:], a.dtype),
        compiler_params=params(),
    )(a, b)


def exchanged(values, orders, k, last, came, deps):
    out = []
    for p, order in enumerate(orders):
        before = list(deps)
        if came is not None:
            before += [came[q] for q in range(len(orders)) if orders[q][last] == order[k]]
        out.append(swapped(tied(values[p], *before) if before else values[p], order[k]))
    return out


def gather_round(held, came, orders, k, deps=()):
    if k > 0:
        held = [join(h, c) for h, c in zip(held, came)]
    return held, exchanged(held, orders, k, k - 1, came, deps)


def sum_cube(keep, send, orders, before):
    keep = [k.astype(f32) for k in keep]
    rounds = len(orders[0])
    came = first = None
    for k in range(rounds - 1, -1, -1):
        came = exchanged(send, orders, k, k + 1, came, before.get(rounds - 1 - k, ()))
        first = came if first is None else first
        total = [a + c.astype(f32) for a, c in zip(keep, came)]
        half = total[0].shape[0] // 2
        if k > 0:
            send = [t[half:].astype(bf16) for t in total]
            keep = [t[:half] for t in total]
    return [t[0].astype(bf16) for t in total], first


def block_place(order, r, z):
    place = 0
    for k, (axis, bit) in enumerate(order):
        on = z if axis == "section" else (r >> bit) & 1
        place = place + (on << k)
    return place


AHEAD = 8
GROUP = 4


def units_of(orders, half, slices, early):
    out = []
    for p, order in enumerate(orders):
        for r in range(slices):
            here = all(block_place(order, r, z) < half for z in range(2))
            if here == early:
                out.append((p, r))
    return out


class Stream:
    def __init__(self):
        self.copies = []

    def add(self, src, dst, sem):
        self.copies.append(pltpu.make_async_copy(src, dst, sem))
        return len(self.copies) - 1

    def begin(self):
        for copy in self.copies[:AHEAD]:
            copy.start()

    def arrived(self, group):
        for i in group:
            self.copies[i].wait()
            if i + AHEAD < len(self.copies):
                self.copies[i + AHEAD].start()


def packed(units, spans):
    starts = [0]
    for p, _ in units:
        starts.append(starts[-1] + spans[p][1] - spans[p][0])
    return starts


def weight_copies(stream, units, feats, mine, gate_ref, up_ref, in_w, sems):
    spans = in_cuts(feats)
    starts = packed(units, spans)
    places = []
    for which, src in enumerate((gate_ref, up_ref)):
        for u, (p, r) in enumerate(units):
            a, b = spans[p]
            row = pl.multiple_of((mine ^ r) * feats + a, 128)
            dst = in_w.at[which, starts[u] : starts[u + 1]]
            sem = sems.at[len(places)]
            places.append(stream.add(src.at[pl.ds(row, b - a)], dst, sem))
    return places


def scale_rows(units, block, gain_ref, scaled, spans, squares):
    for u, (p, r) in enumerate(units):
        a, b = spans[p]
        x = jnp.concatenate([block(p, r, 0), block(p, r, 1)], axis=0).astype(f32)
        scaled[u, :, : b - a] = (x * gain_ref[r, :, a:b]).astype(bf16)
        for c in range(0, b - a, 128):
            squares = squares + x[:, c : c + 128] * x[:, c : c + 128]
    return squares


def product(stream, places, which, units, spans, scaled, in_w, base, n, tile):
    total = base
    starts = packed(units, spans)
    first = which * len(units)
    for u, (p, r) in enumerate(units):
        a, b = spans[p]
        if n == 0 and u % GROUP == 0:
            stream.arrived(places[first + u : first + min(u + GROUP, len(units))])
        term = jnp.dot(
            scaled[u, :, : b - a],
            in_w[which, starts[u] : starts[u + 1], n : n + tile],
            preferred_element_type=f32,
        )
        total = term if total is None else total + term
    return total


def early_kernel(units, orders, feats, me, *refs):
    early = refs[:IN_PARTS]
    gain_ref, gate_ref, up_ref, gate_out, up_out, squares_out = refs[IN_PARTS : IN_PARTS + 6]
    scaled, in_w, sems = refs[IN_PARTS + 6 :]
    rows = early[0].shape[1]
    spans = in_cuts(feats)
    stream = Stream()
    places = weight_copies(stream, units, feats, me[0], gate_ref, up_ref, in_w, sems)
    stream.begin()

    def block(p, r, z):
        return early[p][block_place(orders[p], r, z)]

    squares = jnp.zeros((2 * rows, 128), f32)
    squares_out[...] = scale_rows(units, block, gain_ref, scaled, spans, squares)
    count = gate_out.shape[1]
    tile = min(512, count)
    for first, out in enumerate((gate_out, up_out)):
        for n in range(0, count, tile):
            out[:, n : n + tile] = product(
                stream, places, first, units, spans, scaled, in_w, None, n, tile
            )


def late_kernel(units, orders, sum_orders, out_spans, feats, me, *refs):
    early, late = refs[:IN_PARTS], refs[IN_PARTS : 2 * IN_PARTS]
    refs = refs[2 * IN_PARTS :]
    gain_ref, gate_in, up_in, squares_in, gate_ref, up_ref, down_ref = refs[:7]
    outs = refs[7 : 7 + 2 * OUT_PARTS]
    scaled, hidden, in_w, down_w, sems, down_sems = refs[7 + 2 * OUT_PARTS :]
    half, rows = late[0].shape[:2]
    slices = half
    mine = me[0]
    spans = in_cuts(feats)
    stream = Stream()
    places = weight_copies(stream, units, feats, mine, gate_ref, up_ref, in_w, sems)
    down_places = []
    work = [(p, r) for p in range(OUT_PARTS) for r in range(slices)]
    for p, r in work:
        a, b = out_spans[p]
        col = pl.multiple_of((mine ^ r) * feats + a, 128)
        src = down_ref.at[:, pl.ds(col, b - a)]
        dst = down_w.at[r, :, a:b]
        down_places.append(stream.add(src, dst, down_sems.at[len(down_places)]))
    stream.begin()

    def block(p, r, z):
        place = block_place(orders[p], r, z)
        return early[p][place] if place < half else late[p][place - half]

    squares = scale_rows(units, block, gain_ref, scaled, spans, squares_in[...])
    inv = lax.rsqrt(jnp.sum(squares, axis=1, keepdims=True) / D + norm_eps)
    count = hidden.shape[1]
    tile = min(512, count)
    for n in range(0, count, tile):
        cols = slice(n, n + tile)
        gate = inv * product(
            stream, places, 0, units, spans, scaled, in_w, gate_in[:, cols], n, tile
        )
        up = inv * product(
            stream, places, 1, units, spans, scaled, in_w, up_in[:, cols], n, tile
        )
        hidden[:, cols] = (gate / (1.0 + jnp.exp(-gate)) * up).astype(bf16)

    for i, (p, r) in enumerate(work):
        if i % GROUP == 0:
            stream.arrived(down_places[i : i + GROUP])
        a, b = out_spans[p]
        out = jnp.dot(hidden[...], down_w[r, :, a:b], preferred_element_type=f32).astype(bf16)
        for z in range(2):
            place = block_place(sum_orders[p], r, z)
            part = out[z * rows : (z + 1) * rows]
            outs[2 * p + place // half][place % half] = part


def expert_params():
    return pltpu.CompilerParams(vmem_limit_bytes=40 * 1024 * 1024)


def experts_early(me, early, gain_all, gate_w, up_w, orders):
    half, rows = early[0].shape[:2]
    feats = gain_all.shape[2]
    count = gate_w.shape[1]
    widest = max(b - a for a, b in in_cuts(feats))
    units = units_of(orders, half, half, True)
    vmem = pl.BlockSpec(memory_space=pltpu.VMEM)
    hbm = pl.BlockSpec(memory_space=pltpu.HBM)
    total = jax.ShapeDtypeStruct((2 * rows, count), f32)
    return pl.pallas_call(
        functools.partial(early_kernel, units, orders, feats),
        name="experts_early",
        out_shape=(total, total, jax.ShapeDtypeStruct((2 * rows, 128), f32)),
        in_specs=[pl.BlockSpec(memory_space=pltpu.SMEM)]
        + [vmem] * (IN_PARTS + 1)
        + [hbm] * 2,
        out_specs=[vmem] * 3,
        scratch_shapes=[
            pltpu.VMEM((len(units), 2 * rows, widest), bf16),
            pltpu.VMEM((2, packed(units, in_cuts(feats))[-1], count), bf16),
            pltpu.SemaphoreType.DMA((2 * len(units),)),
        ],
        compiler_params=expert_params(),
        cost_estimate=pl.CostEstimate(
            flops=2 * 2 * rows * D * count,
            bytes_accessed=2 * D * count,
            transcendentals=0,
        ),
    )(me, *early, gain_all, gate_w, up_w)


def experts_late(
    me, early, late, gain_all, sums, gate_w, up_w, down_w, orders, sum_orders, out_spans
):
    half, rows = late[0].shape[:2]
    feats = gain_all.shape[2]
    count = gate_w.shape[1]
    widest = max(b - a for a, b in in_cuts(feats))
    units = units_of(orders, half, half, False)
    vmem = pl.BlockSpec(memory_space=pltpu.VMEM)
    hbm = pl.BlockSpec(memory_space=pltpu.HBM)
    outs = pl.pallas_call(
        functools.partial(late_kernel, units, orders, sum_orders, out_spans, feats),
        name="experts_late",
        out_shape=[
            jax.ShapeDtypeStruct((half, rows, b - a), bf16)
            for a, b in out_spans
            for _ in range(2)
        ],
        in_specs=[pl.BlockSpec(memory_space=pltpu.SMEM)]
        + [vmem] * (2 * IN_PARTS + 4)
        + [hbm] * 3,
        out_specs=[vmem] * (2 * OUT_PARTS),
        scratch_shapes=[
            pltpu.VMEM((len(units), 2 * rows, widest), bf16),
            pltpu.VMEM((2 * rows, count), bf16),
            pltpu.VMEM((2, packed(units, in_cuts(feats))[-1], count), bf16),
            pltpu.VMEM((half, count, feats), bf16),
            pltpu.SemaphoreType.DMA((2 * len(units),)),
            pltpu.SemaphoreType.DMA((half * OUT_PARTS,)),
        ],
        compiler_params=expert_params(),
        cost_estimate=pl.CostEstimate(
            flops=2 * 2 * rows * D * count * 2,
            bytes_accessed=4 * D * count,
            transcendentals=2 * rows * count,
        ),
    )(me, *early, *late, gain_all, *sums, gate_w, up_w, down_w)
    return outs[0::2], outs[1::2]


def tensor_sum(stat):
    for b in range(lax.axis_size("tensor").bit_length() - 1):
        stat = stat + swapped(stat, ("tensor", b))
    return stat


def first_sums(stat, gain_row):
    rows, feats = stat.shape[1], gain_row.shape[1]
    lines = -(-feats // rows)
    gains = jnp.pad(gain_row[0], (0, lines * rows - feats)).reshape(lines, rows)
    steps = []
    for b in range(lax.axis_size("tensor").bit_length() - 1):
        count = 9 + gains.shape[0]
        parcel = jnp.concatenate([stat[:9], gains, jnp.zeros((-count % 8, rows), f32)])
        came = swapped(parcel, ("tensor", b))
        stat = stat[:9] + came[:9]
        gains = jnp.concatenate([gains, came[9:count]])
        steps.append(came)
    gains = gains.reshape(lax.axis_size("tensor"), 1, lines * rows)[:, :, :feats]
    return stat, gains, steps


def on_device(tokens, norm_gain, router, w_gate, w_up, w_down, expert_ids, lengths):
    sections = lax.axis_size("section")
    slices = lax.axis_size("tensor")
    section = lax.axis_index("section")
    core = lax.axis_index("expert").astype(jnp.int32)[None]
    me = lax.axis_index("tensor").astype(jnp.int32)[None]
    layer = section // 2
    rows, feats = tokens.shape
    across = ("expert", 0)

    gain_row = lax.dynamic_index_in_dim(norm_gain, layer, 0, keepdims=True)
    router_t = lax.dynamic_index_in_dim(router, layer, 0, keepdims=False).T
    ids_rows = jnp.transpose(expert_ids, (0, 2, 1))
    place = jnp.stack([core[0], section, (section - 2) % sections]).astype(jnp.int32)
    orders = sum_orders = out_orders(slices)
    rounds = len(orders[0])
    gate_w, up_w, down_w = w_gate[0, 0], w_up[0, 0], w_down[0, 0]
    pieces = []
    begin = 0
    for share in (5, 7, 13, 7):
        pieces.append(tokens[begin : begin + rows * share // 32])
        begin += rows * share // 32

    slots, own, other = prologue(place, lengths, ids_rows, tokens)
    next_slots = ahead(slots, -2)
    blocks = lay(own, swapped(other, across))
    held, came = gather_round(blocks, None, orders, 0)
    stat = stats(tied(tokens, *blocks), gain_row, router_t)
    stat, gain_all, steps = first_sums(stat, gain_row)
    for k in range(1, rounds):
        deps = steps[:1] if k == 1 else [next_slots] if k == rounds - 1 else []
        held, came = gather_round(held, came, orders, k, deps)
    far = [ahead(tied(pieces[0], *held), 2)]
    sums = experts_early(me, held, gain_all, gate_w, up_w, orders)
    aux, base, mix = prepare(core, stat, ids_rows, slots, next_slots, tied(tokens, *held))
    far_aux = ahead(aux, 2)

    came = [tied(c, mix) for c in came]
    far.append(ahead(tied(pieces[1], *came), 2))
    keep, send = experts_late(
        me, held, came, gain_all, sums, gate_w, up_w, down_w, orders, sum_orders, cuts(feats, OUT_PARTS)
    )
    far.append(ahead(tied(pieces[2], *send), 2))
    summed, _ = sum_cube(keep, send, sum_orders, {0: [far[0], far[1]]})

    mine = [s[:CAP] for s in summed]
    theirs = [swapped(s[CAP:], across) for s in summed]
    to_own, to_other, slab_own, slab_other = repick(mix, base, mine, theirs)
    to_own, to_other = tied(to_own, far[2]), tied(to_other, far[2])
    blocks = lay(ahead(to_own, 2), ahead(to_other, 2, True))
    slab_own = ahead(tied(slab_own, *blocks), 2)
    held, came = gather_round(blocks, None, orders, 0)
    for k in range(1, rounds):
        held, came = gather_round(held, came, orders, k, [slab_own] if k == rounds - 1 else [])
    slab_other = ahead(tied(slab_other, *held), 2)
    sums = experts_early(me, held, gain_all, gate_w, up_w, orders)
    came = [tied(c, slab_other) for c in came]
    far.append(ahead(tied(pieces[3], *came), 2))
    keep, send = experts_late(
        me,
        held,
        came,
        gain_all,
        sums,
        gate_w,
        up_w,
        down_w,
        orders,
        sum_orders,
        cuts(feats, OUT_PARTS),
    )

    summed, first = sum_cube(keep, send, sum_orders, {0: [far[3]]})
    far_tokens = jnp.concatenate(far, axis=0)
    far_aux = tied(far_aux, *first)
    state, stat = between(far_tokens, far_aux, slab_own, slab_other, gain_row, router_t)
    stat = tensor_sum(stat)
    mine = [s[:CAP] for s in summed]
    theirs = [swapped(s[CAP:], across) for s in summed]
    return last(core, state, stat, ids_rows, slots, mine, theirs)


def solution(mesh):
    in_specs = (
        P(("section", "expert"), "tensor"),
        P(None, "tensor"),
        P(None, "tensor", None),
        P("section", "expert", None, "tensor"),
        P("section", "expert", None, "tensor"),
        P("section", "expert", "tensor", None),
        P(None, ("section", "expert"), None),
        P(None, "expert"),
    )
    out_specs = P(("section", "expert"), "tensor")
    return jax.shard_map(
        on_device, mesh=mesh, in_specs=in_specs, out_specs=out_specs, check_vma=False
    )
```
